32 devices in a mesh: groups: 2 (over y), ctx: 4 (over x, core), head: 4 (over z).
Axes of the slice: x: 2, y: 2, z: 4, core: 2. Of those that a mesh axis runs over, the one named last changes fastest.
Arguments:
- span_query: bfloat16 [4, 128, 64, 128], P('groups', 'ctx', 'head'), parts along dimension 0, may hold values from -5 to 5
- span_key: bfloat16 [4, 128, 8, 128], P('groups', 'ctx', 'head'), parts along dimension 0, may hold values from -15 to 15
- span_value: bfloat16 [4, 128, 8, 128], P('groups', 'ctx', 'head'), parts along dimension 0, may hold values from -6 to 6
- prefix_key: bfloat16 [64, 128, 8, 128], P(('groups', 'ctx'), None, 'head'), parts along dimension 0, may hold values from -15 to 15
- prefix_value: bfloat16 [64, 128, 8, 128], P(('groups', 'ctx'), None, 'head'), parts along dimension 0, may hold values from -6 to 6
- page_table: int32 [4, 16], P('groups', 'ctx'), parts along dimension 0, may hold values from 0 to 7, as said below
- decode_query: bfloat16 [8, 32, 64, 128], P('groups', 'ctx', 'head'), parts along dimension 0, may hold values from -5 to 5
- decode_key: bfloat16 [8, 32, 8, 128], P('groups', 'ctx', 'head'), parts along dimension 0, may hold values from -15 to 15
- decode_value: bfloat16 [8, 32, 8, 128], P('groups', 'ctx', 'head'), parts along dimension 0, may hold values from -6 to 6
- sample_prompt: int32 [64], P('groups'), parts along dimension 0, may hold values from 0 to 1, as said below
- out_weight: bfloat16 [8192, 8192], P('head', 'ctx'), may hold values from -0.25 to 0.25
Outputs:
- span_out: bfloat16 [4, 128, 8192], P('groups', None, 'ctx'), parts along dimension 0
- decode_out: bfloat16 [8, 32, 8192], P('groups', None, 'ctx'), parts along dimension 0
The draws below stay inside these ranges and needn't reach their ends.
There are 2 independent parts, one for each index of `groups`. The reference program is written for one: setup_inputs(seed, part) draws one part's arguments, and reference() takes and returns one part's arrays. A program takes and returns all parts, laid end to end along the dimension named above; an argument that names none is the same for every part. Nothing has to cross between parts.
Inputs may be any that keep to these rules, and one draw needn't show every extreme that they name: `page_table`: within each block of 4 columns (one index of ctx) the entries of both prompts together are a permutation of 0 to 7. `sample_prompt`: every prompt has exactly 16 samples.
All inputs are finite; a program needn't handle non-finite values.
Results may differ from the reference program's by a relative error of at most 0.0075.
Values may be sent and summed in bfloat16 or wider, within the bound.
A program may use at most 64 MiB of HBM per device.

```python
import jax
import jax.numpy as jnp
from jax import lax

D = 8192
HQ = 64
KVH = 8
HD = 128
PROMPTS = 2
STEPS = 4
PAGE = 128
PAGES_DEV = 4
SPAN = 128
PAGES = 16
PREFIX = 2048
SLOTS = 32
SAMPLES = 32


def base_rows(key, dims):
    return jnp.clip(jax.random.normal(key, dims, jnp.float32), -4.0, 4.0)


def drawn_keys(key, drawn, lead_one, lead_two, salt):
    summed = drawn.reshape(lead_one, lead_two, KVH, HQ // KVH, HD).sum(axis=3)
    jitter = jax.random.normal(jax.random.fold_in(key, salt), (lead_one, lead_two, KVH, HD), jnp.float32)
    return jnp.clip(0.9 * summed + jitter, -15.0, 15.0)


def draw_span_query(key, part):
    drawn = base_rows(jax.random.fold_in(key, 101), (PROMPTS, SPAN, HQ, HD))
    return drawn.astype(jnp.bfloat16)


def draw_span_key(key, part):
    drawn = base_rows(jax.random.fold_in(key, 101), (PROMPTS, SPAN, HQ, HD))
    return drawn_keys(key, drawn, PROMPTS, SPAN, 102).astype(jnp.bfloat16)


def draw_decode_query(key, part):
    drawn = base_rows(jax.random.fold_in(key, 201), (STEPS, SAMPLES, HQ, HD))
    return drawn.astype(jnp.bfloat16)


def draw_decode_key(key, part):
    drawn = base_rows(jax.random.fold_in(key, 201), (STEPS, SAMPLES, HQ, HD))
    return drawn_keys(key, drawn, STEPS, SAMPLES, 202).astype(jnp.bfloat16)


def draw_prefix_key(key, part):
    dims = (SLOTS, PAGE, KVH, HD)
    drawn = jnp.clip(2.5 * jax.random.normal(jax.random.fold_in(key, 501), dims, jnp.float32), -15.0, 15.0)
    return drawn.astype(jnp.bfloat16)


def draw_page_table(key, part):
    shards = PAGES // PAGES_DEV

    def one_shard(shard_id):
        return jax.random.permutation(jax.random.fold_in(key, shard_id + 301), PROMPTS * PAGES_DEV).reshape(PROMPTS, PAGES_DEV)
    blocks = jax.vmap(one_shard)(jnp.arange(shards))
    return blocks.transpose(1, 0, 2).reshape(PROMPTS, PAGES).astype(jnp.int32)


def draw_sample_prompt(key, part):
    return (jax.random.permutation(jax.random.fold_in(key, 401), SAMPLES) % PROMPTS).astype(jnp.int32)


def block_scale(stream_key, shape, pieces, smallest, largest):
    level, own = 1.0, jax.random.fold_in(stream_key, 6)
    for dim, parts in pieces:
        draws = jnp.exp(jax.random.uniform(jax.random.fold_in(own, dim), (parts,), jnp.float32, smallest / len(pieces), largest / len(pieces)))
        level = level * jnp.repeat(draws, shape[dim] // parts).reshape([-1 if axis == dim else 1 for axis in range(len(shape))])
    return level


def bell_draw(stream_key, shape, width, limit, pieces=(), kind=jnp.bfloat16):
    values = width * jax.random.normal(stream_key, shape, jnp.float32)
    if pieces:
        values = values * block_scale(stream_key, shape, pieces, -0.22, 0.18)
    return jnp.clip(values, -limit, limit).astype(kind)


def setup_inputs(seed: int = 0, part: int = 0) -> dict:
    key_list = jax.random.split(jax.random.key(seed), 12)
    part_splits = jax.random.split(jax.random.fold_in(key_list[11], part), 12)
    span_query = draw_span_query(jax.random.fold_in(jax.random.fold_in(key_list[11], part), 71), part)
    span_key = draw_span_key(jax.random.fold_in(jax.random.fold_in(key_list[11], part), 71), part)
    span_value = bell_draw(part_splits[2], (PROMPTS, SPAN, KVH, HD), 1.0, 6.0, ((1, 4), (2, 4)))
    prefix_key = draw_prefix_key(jax.random.fold_in(jax.random.fold_in(key_list[11], part), 71), part)
    prefix_value = bell_draw(part_splits[4], (SLOTS, PAGE, KVH, HD), 1.0, 6.0, ((0, 4), (2, 4)))
    page_table = draw_page_table(jax.random.fold_in(jax.random.fold_in(key_list[11], part), 71), part)
    decode_query = draw_decode_query(jax.random.fold_in(jax.random.fold_in(key_list[11], part), 71), part)
    decode_key = draw_decode_key(jax.random.fold_in(jax.random.fold_in(key_list[11], part), 71), part)
    decode_value = bell_draw(part_splits[8], (STEPS, SAMPLES, KVH, HD), 1.0, 6.0, ((1, 4), (2, 4)))
    sample_prompt = draw_sample_prompt(jax.random.fold_in(jax.random.fold_in(key_list[11], part), 71), part)
    out_weight = bell_draw(key_list[10], (HQ * HD, D), (HQ * HD // 16) ** -0.5, 0.25, ((0, 4), (1, 4)))
    return dict(span_query=span_query, span_key=span_key, span_value=span_value, prefix_key=prefix_key, prefix_value=prefix_value, page_table=page_table, decode_query=decode_query, decode_key=decode_key, decode_value=decode_value, sample_prompt=sample_prompt, out_weight=out_weight)


negative_floor = -1e30


def softmax_rows(scores, allowed, values_here):
    masked = jnp.where(allowed, scores, negative_floor)
    row_max = jnp.max(masked, axis=-1, keepdims=True)
    weights = jnp.exp(masked - row_max)
    weight_sum = jnp.sum(weights, axis=-1, keepdims=True)
    mixed_rows = jnp.dot(weights.astype(jnp.bfloat16), values_here, preferred_element_type=jnp.float32)
    return mixed_rows / weight_sum


def reference(span_query, span_key, span_value, prefix_key, prefix_value, page_table, decode_query, decode_key, decode_value, sample_prompt, out_weight):
    group_size = HQ // KVH
    score_scale = 1.0 / (HD ** 0.5)
    page_index = jnp.arange(PAGES, dtype=jnp.int32)
    slot_index = (page_index // PAGES_DEV * (PROMPTS * PAGES_DEV))[None, :] + page_table
    flat_slots = slot_index.reshape(-1).astype(jnp.int32)
    prompt_keys = jnp.take(prefix_key, flat_slots, axis=0).reshape(PROMPTS, PREFIX, KVH, HD)
    prompt_values = jnp.take(prefix_value, flat_slots, axis=0).reshape(PROMPTS, PREFIX, KVH, HD)
    all_keys = jnp.concatenate([prompt_keys, span_key], axis=1)
    all_values = jnp.concatenate([prompt_values, span_value], axis=1)
    length = PREFIX + SPAN
    key_pos = jnp.arange(length, dtype=jnp.int32)

    head_keys = all_keys.transpose(0, 2, 1, 3).reshape(PROMPTS * KVH, length, HD)
    head_values = all_values.transpose(0, 2, 1, 3).reshape(PROMPTS * KVH, length, HD)
    head_queries = span_query.reshape(PROMPTS, SPAN, KVH, group_size, HD).transpose(0, 2, 1, 3, 4).reshape(PROMPTS * KVH, SPAN * group_size, HD)
    query_pos = jnp.arange(SPAN * group_size, dtype=jnp.int32) // group_size
    allowed = (key_pos[None, :] < PREFIX) | (key_pos[None, :] - PREFIX <= query_pos[:, None])

    def prefill_head(operands):
        queries, keys_here, values_here = operands
        scores = jnp.dot(queries, keys_here.T, preferred_element_type=jnp.float32) * score_scale
        return softmax_rows(scores, allowed, values_here).astype(jnp.bfloat16)

    mixed_heads = lax.map(prefill_head, (head_queries, head_keys, head_values))
    span_attn = mixed_heads.reshape(PROMPTS, KVH, SPAN, group_size, HD).transpose(0, 2, 1, 3, 4).reshape(PROMPTS * SPAN, HQ * HD)

    step_pos = jnp.arange(STEPS * group_size, dtype=jnp.int32) // group_size
    own_allowed = jnp.concatenate([jnp.ones((STEPS * group_size, length), dtype=bool), jnp.arange(STEPS, dtype=jnp.int32)[None, :] <= step_pos[:, None]], axis=1)

    def decode_sample(operands):
        queries, own_keys, own_values, prompt = operands
        keys_here = jnp.concatenate([lax.dynamic_index_in_dim(all_keys, prompt, 0, keepdims=False), own_keys], axis=0)
        values_here = jnp.concatenate([lax.dynamic_index_in_dim(all_values, prompt, 0, keepdims=False), own_values], axis=0)
        grouped = queries.reshape(STEPS, KVH, group_size, HD).transpose(1, 0, 2, 3).reshape(KVH, STEPS * group_size, HD)

        def decode_head(inner_ops):
            one_queries, one_keys, one_values = inner_ops
            scores = jnp.dot(one_queries, one_keys.T, preferred_element_type=jnp.float32) * score_scale
            return softmax_rows(scores, own_allowed, one_values).astype(jnp.bfloat16)

        result = lax.map(decode_head, (grouped, keys_here.transpose(1, 0, 2), values_here.transpose(1, 0, 2)))
        return result.reshape(KVH, STEPS, group_size, HD).transpose(1, 0, 2, 3).reshape(STEPS, HQ * HD)

    decoded = lax.map(decode_sample, (decode_query.transpose(1, 0, 2, 3), decode_key.transpose(1, 0, 2, 3), decode_value.transpose(1, 0, 2, 3), sample_prompt))
    decode_attn = decoded.transpose(1, 0, 2).reshape(STEPS * SAMPLES, HQ * HD)
    span_out = jnp.dot(span_attn, out_weight, preferred_element_type=jnp.float32).astype(jnp.bfloat16).reshape(PROMPTS, SPAN, D)
    decode_out = jnp.dot(decode_attn, out_weight, preferred_element_type=jnp.float32).astype(jnp.bfloat16).reshape(STEPS, SAMPLES, D)
    return span_out, decode_out
```

```python
import functools
import math

import jax
import jax.numpy as jnp
from jax import lax
from jax.experimental import pallas as pl
from jax.experimental.pallas import tpu as pltpu
from jax.sharding import PartitionSpec as P

MESH = pl.DeviceIdType.MESH
F32 = jnp.float32
BF16 = jnp.bfloat16
masked_bias = -1e30


def remote(src, dst, send, recv, device):
    return pltpu.make_async_remote_copy(
        src_ref=src,
        dst_ref=dst,
        send_sem=send,
        recv_sem=recv,
        device_id=device,
        device_id_type=MESH,
    )


def kernel(
    dims,
    table,
    keys_in,
    values_in,
    queries_in,
    small_in,
    bias_in,
    pick_in,
    place_in,
    weight_in,
    out_ref,
    kv_send,
    q_send,
    kv_held,
    q_held,
    attended,
    rows_all,
    decode_rows,
    weight,
    part,
    right_out,
    left_out,
    right_in,
    left_in,
    shared,
    kv_ssem,
    kv_rsem,
    q_ssem,
    q_rsem,
    own_sem,
    sib_ssem,
    far_ssem,
    fwd_ssem,
    att_rsem,
    weight_sem,
    right_ssem,
    right_rsem,
    left_ssem,
    left_rsem,
    agr_ssem,
    agl_ssem,
    ag_rsem,
):
    ctx, heads, prompts, kvh, pages, page, span_dev, dec_dev, qh, pair, picked, groups = dims
    me = lax.axis_index("ctx")
    z = lax.axis_index("head")
    share = ctx // prompts
    hd = 128
    chips = ctx // 2
    prefix = pages * page
    blocks = qh // pair
    span = ctx * span_dev
    gcols = weight.shape[2]
    srows = shared.shape[2]

    for g in range(groups):
        pltpu.make_async_copy(
            weight_in.at[:, g * gcols : (g + 1) * gcols], weight.at[g], weight_sem.at[g]
        ).start()

    barrier = pltpu.get_barrier_semaphore()
    for d in range(1, ctx):
        pl.semaphore_signal(
            barrier, inc=1, device_id={"ctx": lax.rem(me + d, ctx)}, device_id_type=MESH
        )

    @pl.when(z > 0)
    def _():
        pl.semaphore_signal(barrier, inc=1, device_id={"head": z - 1}, device_id_type=MESH)

    @pl.when(z < heads - 1)
    def _():
        pl.semaphore_signal(barrier, inc=1, device_id={"head": z + 1}, device_id_type=MESH)

    for d in range(ctx):
        p, r = d // share, d % share
        cols = slice(r * qh * hd, (r + 1) * qh * hd)
        q_send[d, 0:span_dev] = queries_in[p * span_dev : (p + 1) * span_dev, cols]
        q_send[d, span_dev : span_dev + dec_dev] = queries_in[prompts * span_dev :, cols]
    base = 2 * prefix
    for p in range(prompts):
        for j in range(pages):
            slot = table[p, j]
            key_page = keys_in[slot]
            value_page = values_in[slot]
            for k in range(kvh):
                u = p * kvh + k
                kv_send[u, j * page : (j + 1) * page] = key_page[:, k * hd : (k + 1) * hd]
                kv_send[u, prefix + j * page : prefix + (j + 1) * page] = value_page[
                    :, k * hd : (k + 1) * hd
                ]
        for k in range(kvh):
            u = p * kvh + k
            mine = slice(p * span_dev, (p + 1) * span_dev)
            at = base
            for kind in range(2):
                kv_send[u, at : at + span_dev] = small_in[kind, mine, k * hd : (k + 1) * hd]
                at += span_dev
            for kind in range(2):
                kv_send[u, at : at + dec_dev] = small_in[
                    kind, prompts * span_dev :, k * hd : (k + 1) * hd
                ]
                at += dec_dev

    pl.semaphore_wait(
        barrier, ctx - 1 + jnp.where(z > 0, 1, 0) + jnp.where(z < heads - 1, 1, 0)
    )

    def unit_of(d):
        return d // share * kvh + d % share * kvh // share

    def send_queries(d):
        to = lax.rem(me + d, ctx)
        return remote(q_send.at[to], q_held.at[me], q_ssem.at[d], q_rsem.at[me], {"ctx": to})

    def send_keys(d):
        to = lax.rem(me + d, ctx)
        return remote(
            kv_send.at[unit_of(to)], kv_held.at[me], kv_ssem.at[d], kv_rsem.at[me], {"ctx": to}
        )

    for d in range(1, ctx):
        send_queries(d).start()
    for d in range(1, ctx):
        send_keys(d).start()
    own = (
        pltpu.make_async_copy(q_send.at[me], q_held.at[me], own_sem.at[0]),
        pltpu.make_async_copy(kv_send.at[unit_of(me)], kv_held.at[me], own_sem.at[1]),
    )
    for copy in own:
        copy.start()
    for copy in own:
        copy.wait()
    for d in range(1, ctx):
        at = lax.rem(me + d, ctx)
        remote(q_held.at[at], q_held.at[at], q_ssem.at[d], q_rsem.at[at], {"ctx": at}).wait_recv()
        remote(
            kv_held.at[at], kv_held.at[at], kv_ssem.at[d], kv_rsem.at[at], {"ctx": at}
        ).wait_recv()

    factor = math.log2(math.e) / math.sqrt(hd)
    at = base
    extra = []
    for width in (span_dev, span_dev, dec_dev, dec_dev):
        extra.append([kv_held[c, at : at + width] for c in range(ctx)])
        at += width
    extra_keys = jnp.concatenate(extra[0] + extra[2], axis=0)
    extra_values = jnp.concatenate(extra[1] + extra[3], axis=0)
    dq = jnp.concatenate([q_held[c, span_dev : span_dev + dec_dev] for c in range(ctx)], axis=0)
    dq = jnp.dot(pick_in[...], dq, preferred_element_type=F32).astype(BF16)
    sq = jnp.concatenate([q_held[c, 0:span_dev] for c in range(ctx)], axis=0)
    core_pair = me + 1 - 2 * lax.rem(me, 2)

    def far(e):
        return lax.rem(me + 2 * e, ctx)

    def to_sibling(b):
        return remote(
            attended.at[me, b], attended.at[me, b], sib_ssem.at[b], att_rsem.at[me, b], {"ctx": core_pair}
        )

    def to_far(e, b):
        return remote(
            attended.at[me, b], attended.at[me, b], far_ssem.at[e, b], att_rsem.at[me, b], {"ctx": far(e)}
        )

    def forward(e, b):
        s = far(e)
        return remote(
            attended.at[s, b], attended.at[s, b], fwd_ssem.at[e, b], att_rsem.at[s, b], {"ctx": core_pair}
        )

    def forward_all(b):
        for e in range(1, chips):
            forward(e, b).wait_recv()
            forward(e, b).start()

    def dot_keys(queries, keys):
        return lax.dot_general(queries, keys, (((1,), (1,)), ((), ())), preferred_element_type=F32)

    def attend(queries, bias):
        scores = [dot_keys(queries, kv_held[c, 0:prefix]) for c in range(ctx)]
        last = dot_keys(queries, extra_keys) + bias
        top = jnp.max(last, axis=1, keepdims=True)
        for s in scores:
            top = jnp.maximum(top, jnp.max(s, axis=1, keepdims=True))
        shift = top * factor
        w = jnp.exp2(last * factor - shift)
        total = jnp.sum(w, axis=1, keepdims=True)
        mixed = jnp.dot(w.astype(BF16), extra_values, preferred_element_type=F32)
        for c, s in enumerate(scores):
            w = jnp.exp2(s * factor - shift)
            total = total + jnp.sum(w, axis=1, keepdims=True)
            mixed = mixed + jnp.dot(
                w.astype(BF16), kv_held[c, prefix : 2 * prefix], preferred_element_type=F32
            )
        return (mixed / total).astype(BF16)

    def head_cols(rows, b, i):
        return rows[:, (b * pair + i) * hd : (b * pair + i + 1) * hd]

    for b in range(blocks):
        queries = jnp.concatenate(
            [head_cols(sq, b, i) for i in range(pair)] + [head_cols(dq, b, i) for i in range(pair)],
            axis=0,
        )
        bias = jnp.concatenate([bias_in[0:span]] * pair + [bias_in[span:]] * pair, axis=0)
        total_rows = queries.shape[0]
        slab = total_rows if total_rows <= 512 else 256
        mixed = jnp.concatenate(
            [attend(queries[s : s + slab], bias[s : s + slab]) for s in range(0, total_rows, slab)],
            axis=0,
        )
        for i in range(pair):
            attended[me, b, 0:span, i * hd : (i + 1) * hd] = mixed[i * span : (i + 1) * span]
            start = pair * span + i * picked
            attended[me, b, span : span + picked, i * hd : (i + 1) * hd] = mixed[
                start : start + picked
            ]
        to_sibling(b).start()
        for e in range(1, chips):
            to_far(e, b).start()
        if b > 0:
            forward_all(b - 1)
    forward_all(blocks - 1)

    for d in range(1, ctx):
        send_queries(d).wait_send()
        send_keys(d).wait_send()
    for b in range(blocks):
        to_sibling(b).wait_send()
        for e in range(1, chips):
            to_far(e, b).wait_send()
            forward(e, b).wait_send()
            s = lax.rem(core_pair + 2 * e, ctx)
            remote(
                attended.at[s, b], attended.at[s, b], fwd_ssem.at[e, b], att_rsem.at[s, b], {"ctx": core_pair}
            ).wait_recv()
        remote(
            attended.at[core_pair, b],
            attended.at[core_pair, b],
            sib_ssem.at[b],
            att_rsem.at[core_pair, b],
            {"ctx": core_pair},
        ).wait_recv()

    for d in range(ctx):
        p, r = d // share, d % share
        for b in range(blocks):
            cols = slice((r * qh + b * pair) * hd, (r * qh + (b + 1) * pair) * hd)
            rows_all[p * span : (p + 1) * span, cols] = attended[d, b, 0:span]
            decode_rows[p * picked : (p + 1) * picked, cols] = attended[d, b, span : span + picked]
    rows_all[prompts * span :] = jnp.dot(
        place_in[...], decode_rows[...], preferred_element_type=F32
    ).astype(BF16)

    def shift_right(g, o):
        return remote(
            right_out.at[g, o], right_in.at[g, o], right_ssem.at[g, o], right_rsem.at[g, o], {"head": z + 1}
        )

    def shift_left(g, o):
        return remote(
            left_out.at[g, o], left_in.at[g, o], left_ssem.at[g, o], left_rsem.at[g, o], {"head": z - 1}
        )

    def share_right(g, o):
        return remote(
            shared.at[g, o], shared.at[g, o], agr_ssem.at[g, o], ag_rsem.at[g, o], {"head": z + 1}
        )

    def share_left(g, o):
        return remote(
            shared.at[g, o], shared.at[g, o], agl_ssem.at[g, o], ag_rsem.at[g, o], {"head": z - 1}
        )

    def from_left(g, o):
        remote(
            right_out.at[g, o], right_in.at[g, o], right_ssem.at[g, o], right_rsem.at[g, o], {"head": z - 1}
        ).wait_recv()

    def from_right(g, o):
        remote(
            left_out.at[g, o], left_in.at[g, o], left_ssem.at[g, o], left_rsem.at[g, o], {"head": z + 1}
        ).wait_recv()

    def scatter(g):
        pltpu.make_async_copy(
            weight_in.at[:, g * gcols : (g + 1) * gcols], weight.at[g], weight_sem.at[g]
        ).wait()
        for o in range(heads):
            part[g, o] = jnp.dot(
                rows_all[o * srows : (o + 1) * srows], weight[g], preferred_element_type=F32
            )
        for k in range(heads - 1):
            o = heads - 1 - k

            @pl.when(z == 0)
            def _():
                right_out[g, o] = part[g, o].astype(BF16)
                shift_right(g, o).start()

            @pl.when((z > 0) & (z < o))
            def _():
                from_left(g, o)
                right_out[g, o] = (part[g, o] + right_in[g, o].astype(F32)).astype(BF16)
                shift_right(g, o).start()

            @pl.when(z == heads - 1)
            def _():
                left_out[g, k] = part[g, k].astype(BF16)
                shift_left(g, k).start()

            @pl.when((z < heads - 1) & (z > k))
            def _():
                from_right(g, k)
                left_out[g, k] = (part[g, k] + left_in[g, k].astype(F32)).astype(BF16)
                shift_left(g, k).start()

    def finish(g):
        @pl.when(z == 0)
        def _():
            from_right(g, 0)
            shared[g, 0] = (part[g, 0] + left_in[g, 0].astype(F32)).astype(BF16)
            share_right(g, 0).start()

        @pl.when(z == heads - 1)
        def _():
            o = heads - 1
            from_left(g, o)
            shared[g, o] = (part[g, o] + right_in[g, o].astype(F32)).astype(BF16)
            share_left(g, o).start()

        for o in range(1, heads - 1):

            @pl.when(z == o)
            def _():
                from_left(g, o)
                from_right(g, o)
                shared[g, o] = (
                    part[g, o] + right_in[g, o].astype(F32) + left_in[g, o].astype(F32)
                ).astype(BF16)
                share_right(g, o).start()
                share_left(g, o).start()

    def relay(g):
        for k in range(1, heads):

            @pl.when(z >= k)
            def _():
                o = z - k
                remote(
                    shared.at[g, o], shared.at[g, o], agr_ssem.at[g, o], ag_rsem.at[g, o], {"head": z - 1}
                ).wait_recv()

                @pl.when(z < heads - 1)
                def _():
                    share_right(g, o).start()

            @pl.when(z + k < heads)
            def _():
                o = z + k
                remote(
                    shared.at[g, o], shared.at[g, o], agl_ssem.at[g, o], ag_rsem.at[g, o], {"head": z + 1}
                ).wait_recv()

                @pl.when(z > 0)
                def _():
                    share_left(g, o).start()

        for o in range(heads):
            out_ref[o * srows : (o + 1) * srows, g * gcols : (g + 1) * gcols] = shared[g, o]

    for step in range(groups + 2):
        if step < groups:
            scatter(step)
        if 1 <= step <= groups:
            finish(step - 1)
        if step >= 2:
            relay(step - 2)

    for g in range(groups):
        for o in range(heads):

            @pl.when(z < o)
            def _():
                shift_right(g, o).wait_send()

            @pl.when(z > o)
            def _():
                shift_left(g, o).wait_send()

            @pl.when((o <= z) & (z < heads - 1))
            def _():
                share_right(g, o).wait_send()

            @pl.when((o >= z) & (z > 0))
            def _():
                share_left(g, o).wait_send()


def shards(
    ctx,
    heads,
    span_query,
    span_key,
    span_value,
    prefix_key,
    prefix_value,
    page_table,
    decode_query,
    decode_key,
    decode_value,
    sample_prompt,
    out_weight,
):
    prompts, span_dev, heads_dev, hd = span_query.shape
    kvh = span_key.shape[2]
    steps, samples_dev = decode_query.shape[:2]
    slots, page = prefix_key.shape[:2]
    pages = page_table.shape[1]
    samples = sample_prompt.shape[0]
    each = samples // prompts
    share = ctx // prompts
    qh = heads_dev // share
    pair = min(2, qh)
    dec_dev = steps * samples_dev
    span = ctx * span_dev
    picked = each * steps
    features, columns = out_weight.shape
    rows = prompts * span + steps * samples
    srows = rows // heads
    groups = 4
    gcols = columns // groups
    me = lax.axis_index("ctx")

    queries = jnp.concatenate(
        [
            span_query.reshape(prompts * span_dev, heads_dev * hd),
            decode_query.reshape(dec_dev, heads_dev * hd),
        ],
        axis=0,
    )
    small = jnp.stack(
        [
            jnp.concatenate(
                [s.reshape(prompts * span_dev, kvh * hd), d.reshape(dec_dev, kvh * hd)], axis=0
            )
            for s, d in ((span_key, decode_key), (span_value, decode_value))
        ]
    )
    keys = prefix_key.reshape(slots, page, kvh * hd)
    values = prefix_value.reshape(slots, page, kvh * hd)

    ids = jnp.arange(samples, dtype=jnp.int32)
    before = (ids[None, :] < ids[:, None]) & (sample_prompt[None, :] == sample_prompt[:, None])
    rank = jnp.sum(before.astype(jnp.int32), axis=1)
    chosen = (
        (rank[None, :] == jnp.arange(each, dtype=jnp.int32)[:, None])
        & (sample_prompt == me // share)[None, :]
    ).reshape(each, 1, ctx, 1, samples_dev)
    step_ids = jnp.arange(steps, dtype=jnp.int32)
    row_step = step_ids.reshape(1, steps, 1, 1, 1)
    col_step = step_ids.reshape(1, 1, 1, steps, 1)
    pick = (chosen & (row_step == col_step)).reshape(picked, ctx * dec_dev).astype(BF16)
    own = (chosen & (col_step <= row_step)).reshape(picked, ctx * dec_dev)
    pos = jnp.arange(span, dtype=jnp.int32)
    bias = jnp.concatenate(
        [
            jnp.concatenate(
                [pos[None, :] <= pos[:, None], jnp.zeros((span, ctx * dec_dev), bool)], axis=1
            ),
            jnp.concatenate([jnp.ones((picked, span), bool), own], axis=1),
        ],
        axis=0,
    )
    bias = jnp.where(bias, 0.0, masked_bias).astype(F32)
    target = (sample_prompt * picked + rank * steps)[None, :] + step_ids[:, None]
    place = (
        target.reshape(-1)[:, None] == jnp.arange(prompts * picked, dtype=jnp.int32)[None, :]
    ).astype(BF16)

    dims = (ctx, heads, prompts, kvh, pages, page, span_dev, dec_dev, qh, pair, picked, groups)
    blocks = qh // pair
    kv_rows = 2 * pages * page + 2 * span_dev + 2 * dec_dev
    vmem = pl.BlockSpec(memory_space=pltpu.VMEM)
    dma = pltpu.SemaphoreType.DMA
    sums = (groups, heads, srows, gcols)
    result = pl.pallas_call(
        functools.partial(kernel, dims),
        out_shape=jax.ShapeDtypeStruct((rows, columns), BF16),
        in_specs=[pl.BlockSpec(memory_space=pltpu.SMEM)]
        + [vmem] * 7
        + [pl.BlockSpec(memory_space=pl.ANY)],
        out_specs=vmem,
        scratch_shapes=[
            pltpu.VMEM((prompts * kvh, kv_rows, hd), BF16),
            pltpu.VMEM((ctx, span_dev + dec_dev, qh * hd), BF16),
            pltpu.VMEM((ctx, kv_rows, hd), BF16),
            pltpu.VMEM((ctx, span_dev + dec_dev, qh * hd), BF16),
            pltpu.VMEM((ctx, blocks, span + picked, pair * hd), BF16),
            pltpu.VMEM((rows, features), BF16),
            pltpu.VMEM((prompts * picked, features), BF16),
            pltpu.VMEM((groups, features, gcols), BF16),
            pltpu.VMEM(sums, F32),
            pltpu.VMEM(sums, BF16),
            pltpu.VMEM(sums, BF16),
            pltpu.VMEM(sums, BF16),
            pltpu.VMEM(sums, BF16),
            pltpu.VMEM(sums, BF16),
            dma((ctx,)),
            dma((ctx,)),
            dma((ctx,)),
            dma((ctx,)),
            dma((2,)),
            dma((blocks,)),
            dma((ctx // 2, blocks)),
            dma((ctx // 2, blocks)),
            dma((ctx, blocks)),
            dma((groups,)),
        ]
        + [dma((groups, heads))] * 7,
        compiler_params=pltpu.CompilerParams(
            collective_id=0, has_side_effects=True, vmem_limit_bytes=58 * 1024 * 1024
        ),
        cost_estimate=pl.CostEstimate(
            flops=2 * rows * features * columns, bytes_accessed=16 * 1024 * 1024, transcendentals=0
        ),
    )(page_table, keys, values, queries, small, bias, pick, place, out_weight)
    return (
        result[: prompts * span].reshape(prompts, span, columns),
        result[prompts * span :].reshape(steps, samples, columns),
    )


def solution(mesh):
    return jax.shard_map(
        functools.partial(shards, mesh.shape["ctx"], mesh.shape["head"]),
        mesh=mesh,
        in_specs=(
            P("groups", "ctx", "head", None),
            P("groups", "ctx", "head", None),
            P("groups", "ctx", "head", None),
            P(("groups", "ctx"), None, "head", None),
            P(("groups", "ctx"), None, "head", None),
            P("groups", "ctx"),
            P("groups", "ctx", "head", None),
            P("groups", "ctx", "head", None),
            P("groups", "ctx", "head", None),
            P("groups"),
            P("head", "ctx"),
        ),
        out_specs=(P("groups", None, "ctx"), P("groups", None, "ctx")),
        check_vma=False,
    )
```

```python
import functools
import math

import jax
import jax.numpy as jnp
from jax import lax
from jax.experimental import pallas as pl
from jax.experimental.pallas import tpu as pltpu
from jax.sharding import PartitionSpec as P

MESH = pl.DeviceIdType.MESH
F32 = jnp.float32
BF16 = jnp.bfloat16
masked_bias = -1e30


def div(x, n):
    if n & (n - 1):
        return x // n
    return lax.shift_right_logical(x, jnp.int32(n.bit_length() - 1))


def mod(x, n):
    if n & (n - 1):
        return x % n
    return x & (n - 1)


def iotas(rows, cols):
    shape = (rows, cols)
    return (
        lax.broadcasted_iota(jnp.int32, shape, 0),
        lax.broadcasted_iota(jnp.int32, shape, 1),
    )


def one_hot(mask):
    return jnp.where(mask, 1.0, 0.0).astype(BF16)


def exact(left, right):
    return jnp.dot(left, right, preferred_element_type=F32).astype(BF16)


def heads_first(outer, inner):
    i, j = iotas(outer * inner, outer * inner)
    return one_hot(j == mod(i, outer) * inner + div(i, outer))


def remote(src, dst, send, recv, device):
    return pltpu.make_async_remote_copy(
        src_ref=src,
        dst_ref=dst,
        send_sem=send,
        recv_sem=recv,
        device_id=device,
        device_id_type=MESH,
    )


def kernel(
    dims,
    table,
    prompt_in,
    keys_in,
    values_in,
    span_q_in,
    decode_q_in,
    span_k_in,
    span_v_in,
    decode_k_in,
    decode_v_in,
    weight_in,
    span_out,
    decode_out,
    kv_send,
    q_send,
    kv_held,
    q_held,
    attended,
    block_rows,
    weight,
    part,
    right_out,
    left_out,
    right_in,
    left_in,
    shared,
    summed,
    decode_rows,
    kv_ssem,
    kv_rsem,
    q_ssem,
    q_rsem,
    own_sem,
    sib_ssem,
    far_ssem,
    fwd_ssem,
    att_rsem,
    weight_sem,
    right_ssem,
    right_rsem,
    left_ssem,
    left_rsem,
    agr_ssem,
    agl_ssem,
    ag_rsem,
):
    (
        ctx,
        heads,
        prompts,
        kvh,
        heads_dev,
        pages,
        page,
        span_dev,
        steps,
        samples_dev,
        each,
        qh,
        nb,
        by_cols,
    ) = dims
    me = lax.axis_index("ctx")
    z = lax.axis_index("head")
    share = ctx // prompts
    hd = 128
    chips = ctx // 2
    prefix = pages * page
    dec_dev = steps * samples_dev
    samples = ctx * samples_dev
    span = ctx * span_dev
    picked = each * steps
    sb, pb = span // nb, picked // nb
    groups, unused, crows, ccols = shared.shape

    load_weight = pltpu.make_async_copy(weight_in, weight, weight_sem.at[0])
    load_weight.start()

    barrier = pltpu.get_barrier_semaphore()
    for d in range(1, ctx):
        pl.semaphore_signal(
            barrier, inc=1, device_id={"ctx": lax.rem(me + d, ctx)}, device_id_type=MESH
        )

    @pl.when(z > 0)
    def _():
        pl.semaphore_signal(barrier, inc=1, device_id={"head": z - 1}, device_id_type=MESH)

    @pl.when(z < heads - 1)
    def _():
        pl.semaphore_signal(barrier, inc=1, device_id={"head": z + 1}, device_id_type=MESH)

    order = heads_first(span_dev, heads_dev)
    block = span_dev * heads_dev
    span_rows = [
        exact(order, span_q_in[p * block : (p + 1) * block]) for p in range(prompts)
    ]
    dec_rows = exact(heads_first(dec_dev, heads_dev), decode_q_in[...])
    for d in range(ctx):
        p, r = d // share, d % share
        q_send[d, 0 : qh * span_dev] = span_rows[p][r * qh * span_dev : (r + 1) * qh * span_dev]
        q_send[d, qh * span_dev :] = dec_rows[r * qh * dec_dev : (r + 1) * qh * dec_dev]

    pl.semaphore_wait(
        barrier, ctx - 1 + jnp.where(z > 0, 1, 0) + jnp.where(z < heads - 1, 1, 0)
    )

    def unit_of(d):
        return d // share * kvh + d % share * kvh // share

    def send_queries(d):
        to = lax.rem(me + d, ctx)
        return remote(q_send.at[to], q_held.at[me], q_ssem.at[d], q_rsem.at[me], {"ctx": to})

    def send_keys(d):
        to = lax.rem(me + d, ctx)
        return remote(
            kv_send.at[unit_of(to)], kv_held.at[me], kv_ssem.at[d], kv_rsem.at[me], {"ctx": to}
        )

    for d in range(1, ctx):
        send_queries(d).start()

    def split(outer, keys, values):
        both = jnp.concatenate([keys, values], axis=1)
        if kvh == 1:
            return both
        return exact(heads_first(outer, kvh), both)

    base = 2 * prefix
    for p in range(prompts):
        for j in range(pages):
            slot = table[p, j]
            both = split(page, keys_in[slot], values_in[slot])
            for k in range(kvh):
                u = p * kvh + k
                rows = both[k * page : (k + 1) * page]
                kv_send[u, j * page : (j + 1) * page] = rows[:, :hd]
                kv_send[u, prefix + j * page : prefix + (j + 1) * page] = rows[:, hd:]
        size = span_dev * kvh
        mine = slice(p * size, (p + 1) * size)
        span_both = split(span_dev, span_k_in[mine], span_v_in[mine])
        dec_both = split(dec_dev, decode_k_in[...], decode_v_in[...])
        for k in range(kvh):
            u = p * kvh + k
            at = base
            for both, size in ((span_both, span_dev), (dec_both, dec_dev)):
                rows = both[k * size : (k + 1) * size]
                kv_send[u, at : at + size] = rows[:, :hd]
                kv_send[u, at + size : at + 2 * size] = rows[:, hd:]
                at += 2 * size

    for d in range(1, ctx):
        send_keys(d).start()
    own = (
        pltpu.make_async_copy(q_send.at[me], q_held.at[me], own_sem.at[0]),
        pltpu.make_async_copy(kv_send.at[unit_of(me)], kv_held.at[me], own_sem.at[1]),
    )
    for copy in own:
        copy.start()

    prompt_row = jnp.broadcast_to(prompt_in[...], (8, samples))
    i, j = iotas(samples, samples)
    earlier = one_hot(i < j)
    code = jnp.zeros((8, samples), F32)
    for p in range(prompts):
        here = one_hot(prompt_row == p)
        rank = jnp.dot(here, earlier, preferred_element_type=F32)
        code = code + here.astype(F32) * (rank + p * each)
    code = code.astype(BF16)

    i, j = iotas(samples, ctx * dec_dev)
    spread = one_hot(i == div(j, dec_dev) * samples_dev + mod(j, samples_dev))
    col_code = jnp.dot(code, spread, preferred_element_type=F32)[0:1]
    i, j = iotas(picked, ctx * dec_dev)
    wanted = (div(i, steps) + me // share * each).astype(F32)
    same = jnp.where(col_code == wanted, 1, 0)
    later = mod(i, steps) - mod(div(j, samples_dev), steps)
    pick = one_hot((same == 1) & (later == 0))
    own_bias = jnp.where((same == 1) & (later >= 0), 0.0, masked_bias)
    i, j = iotas(span, span)
    span_bias = jnp.where(j <= i, 0.0, masked_bias)

    for copy in own:
        copy.wait()
    for d in range(1, ctx):
        at = lax.rem(me + d, ctx)
        remote(q_held.at[at], q_held.at[at], q_ssem.at[d], q_rsem.at[at], {"ctx": at}).wait_recv()
    dq = jnp.concatenate(
        [
            jnp.concatenate(
                [
                    q_held[c, qh * span_dev + g * dec_dev : qh * span_dev + (g + 1) * dec_dev]
                    for c in range(ctx)
                ],
                axis=0,
            )
            for g in range(qh)
        ],
        axis=1,
    )
    dq = exact(pick, dq)
    for d in range(1, ctx):
        at = lax.rem(me + d, ctx)
        remote(
            kv_held.at[at], kv_held.at[at], kv_ssem.at[d], kv_rsem.at[at], {"ctx": at}
        ).wait_recv()

    factor = math.log2(math.e) / math.sqrt(hd)
    at = base
    extra = []
    for width in (span_dev, span_dev, dec_dev, dec_dev):
        extra.append([kv_held[c, at : at + width] for c in range(ctx)])
        at += width
    extra_keys = jnp.concatenate(extra[0] + extra[2], axis=0)
    extra_values = jnp.concatenate(extra[1] + extra[3], axis=0)
    core_pair = me + 1 - 2 * lax.rem(me, 2)

    def far(e):
        return lax.rem(me + 2 * e, ctx)

    def gather_copy(source, b, sem, to):
        rows = attended.at[source, b]
        return remote(rows, rows, sem, att_rsem.at[source, b], {"ctx": to})

    def to_sibling(b):
        return gather_copy(me, b, sib_ssem.at[b], core_pair)

    def to_far(e, b):
        return gather_copy(me, b, far_ssem.at[e, b], far(e))

    def forward(e, b):
        return gather_copy(far(e), b, fwd_ssem.at[e, b], core_pair)

    def forward_all(b):
        for e in range(1, chips):
            forward(e, b).wait_recv()
            forward(e, b).start()

    def dot_keys(queries, keys):
        return lax.dot_general(queries, keys, (((1,), (1,)), ((), ())), preferred_element_type=F32)

    def attend(queries, bias):
        scores = [dot_keys(queries, kv_held[c, 0:prefix]) for c in range(ctx)]
        last = dot_keys(queries, extra_keys) + bias
        top = jnp.max(last, axis=1, keepdims=True)
        for s in scores:
            top = jnp.maximum(top, jnp.max(s, axis=1, keepdims=True))
        shift = top * factor
        w = jnp.exp2(last * factor - shift)
        total = jnp.sum(w, axis=1, keepdims=True)
        mixed = jnp.dot(w.astype(BF16), extra_values, preferred_element_type=F32)
        for c, s in enumerate(scores):
            w = jnp.exp2(s * factor - shift)
            total = total + jnp.sum(w, axis=1, keepdims=True)
            mixed = mixed + jnp.dot(
                w.astype(BF16), kv_held[c, prefix : 2 * prefix], preferred_element_type=F32
            )
        return (mixed / total).astype(BF16)

    per_block = ctx // nb

    def attend_half(b, half):
        split_at = (qh + 1) // 2
        chosen = range(0, split_at) if half == 0 else range(split_at, qh)
        count = len(chosen)
        if count == 0:
            return
        sources = range(b * per_block, (b + 1) * per_block)
        queries = [
            q_held[c, g * span_dev : (g + 1) * span_dev] for g in chosen for c in sources
        ] + [dq[b * pb : (b + 1) * pb, g * hd : (g + 1) * hd] for g in chosen]
        span_part = jnp.concatenate(
            [span_bias[b * sb : (b + 1) * sb], jnp.full((sb, ctx * dec_dev), masked_bias, F32)],
            axis=1,
        )
        dec_part = jnp.concatenate(
            [jnp.zeros((pb, span), F32), own_bias[b * pb : (b + 1) * pb]], axis=1
        )
        bias = jnp.concatenate([span_part] * count + [dec_part] * count, axis=0)
        mixed = attend(jnp.concatenate(queries, axis=0), bias)
        for n, g in enumerate(chosen):
            cols = slice(g * hd, (g + 1) * hd)
            attended[me, b, 0:sb, cols] = mixed[n * sb : (n + 1) * sb]
            start = count * sb + n * pb
            attended[me, b, sb : sb + pb, cols] = mixed[start : start + pb]

    def collect(b):
        gather_copy(core_pair, b, sib_ssem.at[b], core_pair).wait_recv()
        for e in range(1, chips):
            gather_copy(
                lax.rem(core_pair + 2 * e, ctx), b, fwd_ssem.at[e, b], core_pair
            ).wait_recv()
        for d in range(ctx):
            p, r = d // share, d % share
            cols = slice(r * qh * hd, (r + 1) * qh * hd)
            block_rows[b, p * sb : (p + 1) * sb, cols] = attended[d, b, 0:sb]
            start = prompts * sb + p * pb
            block_rows[b, start : start + pb, cols] = attended[d, b, sb : sb + pb]

    def piece(g, o):
        b, half = g // 2, g % 2
        row = 0 if by_cols else o * crows
        col = (2 * o + half if by_cols else half) * ccols
        return b, slice(row, row + crows), slice(col, col + ccols)

    def shift_right(g, o, to):
        return remote(
            right_out.at[g, o], right_in.at[g, o], right_ssem.at[g, o], right_rsem.at[g, o], {"head": to}
        )

    def shift_left(g, o, to):
        return remote(
            left_out.at[g, o], left_in.at[g, o], left_ssem.at[g, o], left_rsem.at[g, o], {"head": to}
        )

    def share_right(g, o, to):
        rows = shared.at[g, o]
        return remote(rows, rows, agr_ssem.at[g, o], ag_rsem.at[g, o], {"head": to})

    def share_left(g, o, to):
        rows = shared.at[g, o]
        return remote(rows, rows, agl_ssem.at[g, o], ag_rsem.at[g, o], {"head": to})

    def when_group(g):
        return pl.when((g >= 0) & (g < groups))

    def project(g):
        for o in range(heads):
            b, rows, cols = piece(g, o)
            part[g, o] = jnp.dot(
                block_rows[b, rows], weight[:, cols], preferred_element_type=F32
            )

    def hop(tick):
        g = tick - z

        @when_group(g)
        def _():
            for o in range(heads - 1, 0, -1):

                @pl.when(z == 0)
                def _():
                    right_out[g, o] = part[g, o].astype(BF16)
                    shift_right(g, o, z + 1).start()

                @pl.when((z > 0) & (z < o))
                def _():
                    shift_right(g, o, z - 1).wait_recv()
                    right_out[g, o] = (part[g, o] + right_in[g, o].astype(F32)).astype(BF16)
                    shift_right(g, o, z + 1).start()

        h = tick - (heads - 1 - z)

        @when_group(h)
        def _():
            for o in range(heads - 1):

                @pl.when(z == heads - 1)
                def _():
                    left_out[h, o] = part[h, o].astype(BF16)
                    shift_left(h, o, z - 1).start()

                @pl.when((z < heads - 1) & (z > o))
                def _():
                    shift_left(h, o, z + 1).wait_recv()
                    left_out[h, o] = (part[h, o] + left_in[h, o].astype(F32)).astype(BF16)
                    shift_left(h, o, z - 1).start()

    def ready(o):
        return jnp.maximum(o, heads - 1 - o)

    def finish(tick):
        g = tick - ready(z)

        @when_group(g)
        def _():
            @pl.when(z == 0)
            def _():
                shift_left(g, z, z + 1).wait_recv()
                shared[g, z] = (part[g, z] + left_in[g, z].astype(F32)).astype(BF16)
                share_right(g, z, z + 1).start()

            @pl.when(z == heads - 1)
            def _():
                shift_right(g, z, z - 1).wait_recv()
                shared[g, z] = (part[g, z] + right_in[g, z].astype(F32)).astype(BF16)
                share_left(g, z, z - 1).start()

            @pl.when((z > 0) & (z < heads - 1))
            def _():
                shift_right(g, z, z - 1).wait_recv()
                shift_left(g, z, z + 1).wait_recv()
                shared[g, z] = (
                    part[g, z] + right_in[g, z].astype(F32) + left_in[g, z].astype(F32)
                ).astype(BF16)
                share_right(g, z, z + 1).start()
                share_left(g, z, z - 1).start()

    def relay(tick):
        for k in range(1, heads):
            o = z - k
            g = tick - ready(o) - k

            @pl.when((o >= 0) & (g >= 0) & (g < groups))
            def _():
                share_right(g, o, z - 1).wait_recv()

                @pl.when(z < heads - 1)
                def _():
                    share_right(g, o, z + 1).start()

            q = z + k
            h = tick - ready(q) - k

            @pl.when((q < heads) & (h >= 0) & (h < groups))
            def _():
                share_left(h, q, z + 1).wait_recv()

                @pl.when(z > 0)
                def _():
                    share_left(h, q, z - 1).start()

    def tick(t):
        if t < groups:
            project(t)
        hop(t)
        finish(t)
        relay(t)

    for b in range(nb):
        attend_half(b, 0)
        if b == 0:
            load_weight.wait()
        if b >= 1:
            forward_all(b - 1)
        if b >= 2:
            tick(2 * (b - 2) + 1)
        attend_half(b, 1)
        to_sibling(b).start()
        for e in range(1, chips):
            to_far(e, b).start()
        if b >= 1:
            collect(b - 1)
            tick(2 * (b - 1))
    forward_all(nb - 1)
    tick(2 * (nb - 2) + 1)
    collect(nb - 1)
    for t in range(2 * (nb - 1), groups + 2 * (heads - 1)):
        tick(t)

    for g in range(groups):
        for o in range(heads):
            b, rows, cols = piece(g, o)
            summed[b, rows, cols] = shared[g, o]
    for b in range(nb):
        for p in range(prompts):
            span_out[p * span + b * sb : p * span + (b + 1) * sb] = summed[b, p * sb : (p + 1) * sb]
            start = prompts * sb + p * pb
            decode_rows[p * picked + b * pb : p * picked + (b + 1) * pb] = summed[
                b, start : start + pb
            ]
    i, j = iotas(samples, steps * samples)
    col_code = jnp.dot(code, one_hot(i == mod(j, samples)), preferred_element_type=F32)[0:1]
    i, j = iotas(prompts * picked, steps * samples)
    same = jnp.where(col_code == div(i, steps).astype(F32), 1, 0)
    place = one_hot((same == 1) & (div(j, samples) == mod(i, steps)))
    decode_out[...] = lax.dot_general(
        place, decode_rows[...], (((0,), (0,)), ((), ())), preferred_element_type=F32
    ).astype(BF16)

    for d in range(1, ctx):
        send_queries(d).wait_send()
        send_keys(d).wait_send()
    for b in range(nb):
        to_sibling(b).wait_send()
        for e in range(1, chips):
            to_far(e, b).wait_send()
            forward(e, b).wait_send()
    for g in range(groups):
        for o in range(heads):

            @pl.when(z < o)
            def _():
                shift_right(g, o, z + 1).wait_send()

            @pl.when(z > o)
            def _():
                shift_left(g, o, z - 1).wait_send()

            @pl.when((o <= z) & (z < heads - 1))
            def _():
                share_right(g, o, z + 1).wait_send()

            @pl.when((o >= z) & (z > 0))
            def _():
                share_left(g, o, z - 1).wait_send()


def shards(
    ctx,
    heads,
    span_query,
    span_key,
    span_value,
    prefix_key,
    prefix_value,
    page_table,
    decode_query,
    decode_key,
    decode_value,
    sample_prompt,
    out_weight,
):
    prompts, span_dev, heads_dev, hd = span_query.shape
    kvh = span_key.shape[2]
    steps, samples_dev = decode_query.shape[:2]
    slots, page = prefix_key.shape[:2]
    pages = page_table.shape[1]
    samples = sample_prompt.shape[0]
    each = samples // prompts
    qh = heads_dev * prompts // ctx
    dec_dev = steps * samples_dev
    span = ctx * span_dev
    picked = each * steps
    features, columns = out_weight.shape
    nb = 4
    groups = 2 * nb
    brows = (prompts * span + steps * samples) // nb
    by_cols = columns // heads >= 256
    crows = brows if by_cols else brows // heads
    ccols = (columns // heads if by_cols else columns) // 2

    dims = (
        ctx,
        heads,
        prompts,
        kvh,
        heads_dev,
        pages,
        page,
        span_dev,
        steps,
        samples_dev,
        each,
        qh,
        nb,
        by_cols,
    )
    kv_rows = 2 * pages * page + 2 * span_dev + 2 * dec_dev
    q_rows = qh * (span_dev + dec_dev)
    vmem = pl.BlockSpec(memory_space=pltpu.VMEM)
    dma = pltpu.SemaphoreType.DMA
    sums = (groups, heads, crows, ccols)
    span_out, decode_out = pl.pallas_call(
        functools.partial(kernel, dims),
        out_shape=(
            jax.ShapeDtypeStruct((prompts * span, columns), BF16),
            jax.ShapeDtypeStruct((steps * samples, columns), BF16),
        ),
        in_specs=[pl.BlockSpec(memory_space=pltpu.SMEM)]
        + [vmem] * 9
        + [pl.BlockSpec(memory_space=pl.ANY)],
        out_specs=(vmem, vmem),
        scratch_shapes=[
            pltpu.VMEM((prompts * kvh, kv_rows, hd), BF16),
            pltpu.VMEM((ctx, q_rows, hd), BF16),
            pltpu.VMEM((ctx, kv_rows, hd), BF16),
            pltpu.VMEM((ctx, q_rows, hd), BF16),
            pltpu.VMEM((ctx, nb, (span + picked) // nb, qh * hd), BF16),
            pltpu.VMEM((nb, brows, features), BF16),
            pltpu.VMEM((features, columns), BF16),
            pltpu.VMEM(sums, F32),
            pltpu.VMEM(sums, BF16),
            pltpu.VMEM(sums, BF16),
            pltpu.VMEM(sums, BF16),
            pltpu.VMEM(sums, BF16),
            pltpu.VMEM(sums, BF16),
            pltpu.VMEM((nb, brows, columns), BF16),
            pltpu.VMEM((prompts * picked, columns), BF16),
            dma((ctx,)),
            dma((ctx,)),
            dma((ctx,)),
            dma((ctx,)),
            dma((2,)),
            dma((nb,)),
            dma((ctx // 2, nb)),
            dma((ctx // 2, nb)),
            dma((ctx, nb)),
            dma((1,)),
        ]
        + [dma((groups, heads))] * 7,
        compiler_params=pltpu.CompilerParams(
            collective_id=0, has_side_effects=True, vmem_limit_bytes=58 * 1024 * 1024
        ),
        cost_estimate=pl.CostEstimate(
            flops=2 * prompts * span * features * columns,
            bytes_accessed=16 * 1024 * 1024,
            transcendentals=0,
        ),
    )(
        page_table,
        sample_prompt.reshape(1, samples),
        prefix_key.reshape(slots, page * kvh, hd),
        prefix_value.reshape(slots, page * kvh, hd),
        span_query.reshape(-1, hd),
        decode_query.reshape(-1, hd),
        span_key.reshape(-1, hd),
        span_value.reshape(-1, hd),
        decode_key.reshape(-1, hd),
        decode_value.reshape(-1, hd),
        out_weight,
    )
    return (
        span_out.reshape(prompts, span, columns),
        decode_out.reshape(steps, samples, columns),
    )


def solution(mesh):
    return jax.shard_map(
        functools.partial(shards, mesh.shape["ctx"], mesh.shape["head"]),
        mesh=mesh,
        in_specs=(
            P("groups", "ctx", "head", None),
            P("groups", "ctx", "head", None),
            P("groups", "ctx", "head", None),
            P(("groups", "ctx"), None, "head", None),
            P(("groups", "ctx"), None, "head", None),
            P("groups", "ctx"),
            P("groups", "ctx", "head", None),
            P("groups", "ctx", "head", None),
            P("groups", "ctx", "head", None),
            P("groups"),
            P("head", "ctx"),
        ),
        out_specs=(P("groups", None, "ctx"), P("groups", None, "ctx")),
        check_vma=False,
    )
```

```python
import functools
import math

import jax
import jax.numpy as jnp
from jax import lax
from jax.experimental import pallas as pl
from jax.experimental.pallas import tpu as pltpu
from jax.sharding import PartitionSpec as P

MESH = pl.DeviceIdType.MESH
F32 = jnp.float32
BF16 = jnp.bfloat16
masked_bias = -1e30


def div(x, n):
    if n & (n - 1):
        return x // n
    return lax.shift_right_logical(x, jnp.int32(n.bit_length() - 1))


def mod(x, n):
    if n & (n - 1):
        return x % n
    return x & (n - 1)


def iotas(rows, cols):
    shape = (rows, cols)
    return (
        lax.broadcasted_iota(jnp.int32, shape, 0),
        lax.broadcasted_iota(jnp.int32, shape, 1),
    )


def one_hot(mask):
    return jnp.where(mask, 1.0, 0.0).astype(BF16)


def exact(left, right):
    return jnp.dot(left, right, preferred_element_type=F32).astype(BF16)


def heads_first(outer, inner):
    i, j = iotas(outer * inner, outer * inner)
    return one_hot(j == mod(i, outer) * inner + div(i, outer))


def remote(src, dst, send, recv, device):
    return pltpu.make_async_remote_copy(
        src_ref=src,
        dst_ref=dst,
        send_sem=send,
        recv_sem=recv,
        device_id=device,
        device_id_type=MESH,
    )


def kernel(
    dims,
    table,
    prompt_in,
    keys_in,
    values_in,
    span_q_in,
    decode_q_in,
    span_k_in,
    span_v_in,
    decode_k_in,
    decode_v_in,
    weight_in,
    summed,
    place_out,
    kv_send,
    q_send,
    kv_held,
    q_held,
    attended,
    block_rows,
    weight,
    part,
    right_out,
    left_out,
    right_in,
    left_in,
    shared,
    kv_ssem,
    kv_rsem,
    q_ssem,
    q_rsem,
    s_ssem,
    s_rsem,
    own_sem,
    sib_ssem,
    far_ssem,
    fwd_ssem,
    att_rsem,
    weight_sem,
    right_ssem,
    right_rsem,
    left_ssem,
    left_rsem,
    agr_ssem,
    agl_ssem,
    ag_rsem,
    done_sem,
):
    (
        ctx,
        heads,
        prompts,
        kvh,
        heads_dev,
        pages,
        page,
        span_dev,
        steps,
        samples_dev,
        each,
        qh,
        nb,
        by_cols,
    ) = dims
    me = lax.axis_index("ctx")
    z = lax.axis_index("head")
    share = ctx // prompts
    hd = 128
    chips = ctx // 2
    prefix = pages * page
    dec_dev = steps * samples_dev
    samples = ctx * samples_dev
    span = ctx * span_dev
    picked = each * steps
    sb, pb = span // nb, picked // nb
    groups, unused, crows, ccols = shared.shape

    load_weight = pltpu.make_async_copy(weight_in, weight, weight_sem.at[0])
    load_weight.start()

    barrier = pltpu.get_barrier_semaphore()
    for d in range(1, ctx):
        pl.semaphore_signal(
            barrier, inc=1, device_id={"ctx": lax.rem(me + d, ctx)}, device_id_type=MESH
        )

    @pl.when(z > 0)
    def _():
        pl.semaphore_signal(barrier, inc=1, device_id={"head": z - 1}, device_id_type=MESH)

    @pl.when(z < heads - 1)
    def _():
        pl.semaphore_signal(barrier, inc=1, device_id={"head": z + 1}, device_id_type=MESH)

    order = heads_first(span_dev, heads_dev)
    block = span_dev * heads_dev
    span_rows = [
        exact(order, span_q_in[p * block : (p + 1) * block]) for p in range(prompts)
    ]
    dec_rows = exact(heads_first(dec_dev, heads_dev), decode_q_in[...])
    for d in range(ctx):
        p, r = d // share, d % share
        q_send[d, 0 : qh * span_dev] = span_rows[p][r * qh * span_dev : (r + 1) * qh * span_dev]
        q_send[d, qh * span_dev :] = dec_rows[r * qh * dec_dev : (r + 1) * qh * dec_dev]

    pl.semaphore_wait(
        barrier, ctx - 1 + jnp.where(z > 0, 1, 0) + jnp.where(z < heads - 1, 1, 0)
    )

    def unit_of(d):
        return d // share * kvh + d % share * kvh // share

    core_pair = me + 1 - 2 * lax.rem(me, 2)
    q_span = pl.ds(0, qh * span_dev)
    q_dec = pl.ds(qh * span_dev, qh * dec_dev)

    def send_queries(d):
        to = lax.rem(me + d, ctx)
        return remote(
            q_send.at[to, q_dec], q_held.at[me, q_dec], q_ssem.at[d], q_rsem.at[me], {"ctx": to}
        )

    def send_span(d):
        to = lax.rem(me + d, ctx)
        return remote(
            q_send.at[to, q_span], q_held.at[me, q_span], s_ssem.at[d], s_rsem.at[me], {"ctx": to}
        )

    def send_keys(d):
        to = lax.rem(me + d, ctx)
        return remote(
            kv_send.at[unit_of(to)], kv_held.at[me], kv_ssem.at[d], kv_rsem.at[me], {"ctx": to}
        )

    for d in range(1, ctx):
        send_queries(d).start()

        @pl.when(lax.rem(me + d, ctx) == core_pair)
        def _():
            send_span(d).start()

    def split(outer, keys, values):
        both = jnp.concatenate([keys, values], axis=1)
        if kvh == 1:
            return both
        return exact(heads_first(outer, kvh), both)

    base = 2 * prefix
    for p in range(prompts):
        for j in range(pages):
            slot = table[p, j]
            both = split(page, keys_in[slot], values_in[slot])
            for k in range(kvh):
                u = p * kvh + k
                rows = both[k * page : (k + 1) * page]
                kv_send[u, j * page : (j + 1) * page] = rows[:, :hd]
                kv_send[u, prefix + j * page : prefix + (j + 1) * page] = rows[:, hd:]
        size = span_dev * kvh
        mine = slice(p * size, (p + 1) * size)
        span_both = split(span_dev, span_k_in[mine], span_v_in[mine])
        dec_both = split(dec_dev, decode_k_in[...], decode_v_in[...])
        for k in range(kvh):
            u = p * kvh + k
            at = base
            for both, size in ((span_both, span_dev), (dec_both, dec_dev)):
                rows = both[k * size : (k + 1) * size]
                kv_send[u, at : at + size] = rows[:, :hd]
                kv_send[u, at + size : at + 2 * size] = rows[:, hd:]
                at += 2 * size

    for d in range(1, ctx):
        send_keys(d).start()
    own = (
        pltpu.make_async_copy(q_send.at[me], q_held.at[me], own_sem.at[0]),
        pltpu.make_async_copy(kv_send.at[unit_of(me)], kv_held.at[me], own_sem.at[1]),
    )
    for copy in own:
        copy.start()

    prompt_row = jnp.broadcast_to(prompt_in[...], (8, samples))
    i, j = iotas(samples, samples)
    earlier = one_hot(i < j)
    code = jnp.zeros((8, samples), F32)
    for p in range(prompts):
        here = one_hot(prompt_row == p)
        rank = jnp.dot(here, earlier, preferred_element_type=F32)
        code = code + here.astype(F32) * (rank + p * each)
    code = code.astype(BF16)

    i, j = iotas(samples, ctx * dec_dev)
    spread = one_hot(i == div(j, dec_dev) * samples_dev + mod(j, samples_dev))
    col_code = jnp.dot(code, spread, preferred_element_type=F32)[0:1]
    i, j = iotas(picked, ctx * dec_dev)
    wanted = (div(i, steps) + me // share * each).astype(F32)
    same = jnp.where(col_code == wanted, 1, 0)
    later = mod(i, steps) - mod(div(j, samples_dev), steps)
    pick = one_hot((same == 1) & (later == 0))
    own_bias = jnp.where((same == 1) & (later >= 0), 0.0, masked_bias)

    i, j = iotas(samples, steps * samples)
    col_code = jnp.dot(code, one_hot(i == mod(j, samples)), preferred_element_type=F32)[0:1]
    i, j = iotas(prompts * picked, steps * samples)
    same = jnp.where(col_code == div(i, steps).astype(F32), 1, 0)
    place_out[...] = one_hot((same == 1) & (div(j, samples) == mod(i, steps)))

    for copy in own:
        copy.wait()
    for d in range(1, ctx):
        at = lax.rem(me + d, ctx)
        rows = q_held.at[at, q_dec]
        remote(rows, rows, q_ssem.at[d], q_rsem.at[at], {"ctx": at}).wait_recv()
    dq = jnp.concatenate(
        [
            jnp.concatenate(
                [
                    q_held[c, qh * span_dev + g * dec_dev : qh * span_dev + (g + 1) * dec_dev]
                    for c in range(ctx)
                ],
                axis=0,
            )
            for g in range(qh)
        ],
        axis=1,
    )
    dq = exact(pick, dq)
    for d in range(1, ctx):
        at = lax.rem(me + d, ctx)
        remote(
            kv_held.at[at], kv_held.at[at], kv_ssem.at[d], kv_rsem.at[at], {"ctx": at}
        ).wait_recv()
    for d in range(1, ctx):

        @pl.when(lax.rem(me + d, ctx) != core_pair)
        def _():
            send_span(d).start()

    factor = math.log2(math.e) / math.sqrt(hd)
    at = base
    extra = []
    for width in (span_dev, span_dev, dec_dev, dec_dev):
        extra.append([kv_held[c, at : at + width] for c in range(ctx)])
        at += width
    extra_keys = jnp.concatenate(extra[0] + extra[2], axis=0)
    extra_values = jnp.concatenate(extra[1] + extra[3], axis=0)

    def far(e):
        return lax.rem(me + 2 * e, ctx)

    def gather_copy(source, b, sem, to):
        rows = attended.at[source, b]
        return remote(rows, rows, sem, att_rsem.at[source, b], {"ctx": to})

    def to_sibling(b):
        return gather_copy(me, b, sib_ssem.at[b], core_pair)

    def to_far(e, b):
        return gather_copy(me, b, far_ssem.at[e, b], far(e))

    def forward(e, b):
        return gather_copy(far(e), b, fwd_ssem.at[e, b], core_pair)

    def forward_all(b):
        for e in range(1, chips):
            forward(e, b).wait_recv()
            forward(e, b).start()

    def dot_keys(queries, keys):
        return lax.dot_general(queries, keys, (((1,), (1,)), ((), ())), preferred_element_type=F32)

    def attend(queries, bias):
        scores = [dot_keys(queries, kv_held[c, 0:prefix]) for c in range(ctx)]
        last = dot_keys(queries, extra_keys) + bias
        top = jnp.max(last, axis=1, keepdims=True)
        for s in scores:
            top = jnp.maximum(top, jnp.max(s, axis=1, keepdims=True))
        shift = top * factor
        w = jnp.exp2(last * factor - shift)
        total = jnp.sum(w, axis=1, keepdims=True)
        mixed = jnp.dot(w.astype(BF16), extra_values, preferred_element_type=F32)
        for c, s in enumerate(scores):
            w = jnp.exp2(s * factor - shift)
            total = total + jnp.sum(w, axis=1, keepdims=True)
            mixed = mixed + jnp.dot(
                w.astype(BF16), kv_held[c, prefix : 2 * prefix], preferred_element_type=F32
            )
        return (mixed / total).astype(BF16)

    per_block = ctx // nb

    def attend_half(b, half):
        split_at = (qh + 1) // 2
        chosen = range(0, split_at) if half == 0 else range(split_at, qh)
        count = len(chosen)
        if count == 0:
            return
        sources = [
            lax.rem(me // share * share + b * per_block + n, ctx) for n in range(per_block)
        ]
        if half == 0:
            for c in sources:

                @pl.when(c != me)
                def _():
                    rows = q_held.at[c, q_span]
                    remote(rows, rows, s_ssem.at[0], s_rsem.at[c], {"ctx": c}).wait_recv()

        queries = [
            q_held[c, g * span_dev : (g + 1) * span_dev] for g in chosen for c in sources
        ] + [dq[b * pb : (b + 1) * pb, g * hd : (g + 1) * hd] for g in chosen]
        i, j = iotas(span_dev, span)
        span_part = jnp.concatenate(
            [
                jnp.concatenate(
                    [
                        jnp.where(j <= i + c * span_dev, 0.0, masked_bias),
                        jnp.full((span_dev, ctx * dec_dev), masked_bias, F32),
                    ],
                    axis=1,
                )
                for c in sources
            ],
            axis=0,
        )
        dec_part = jnp.concatenate(
            [jnp.zeros((pb, span), F32), own_bias[b * pb : (b + 1) * pb]], axis=1
        )
        bias = jnp.concatenate([span_part] * count + [dec_part] * count, axis=0)
        mixed = attend(jnp.concatenate(queries, axis=0), bias)
        for n, g in enumerate(chosen):
            cols = slice(g * hd, (g + 1) * hd)
            attended[me, b, 0:sb, cols] = mixed[n * sb : (n + 1) * sb]
            start = count * sb + n * pb
            attended[me, b, sb : sb + pb, cols] = mixed[start : start + pb]

    def collect(b):
        gather_copy(core_pair, b, sib_ssem.at[b], core_pair).wait_recv()
        for e in range(1, chips):
            gather_copy(
                lax.rem(core_pair + 2 * e, ctx), b, fwd_ssem.at[e, b], core_pair
            ).wait_recv()
        for d in range(ctx):
            p, r = d // share, d % share
            cols = slice(r * qh * hd, (r + 1) * qh * hd)
            block_rows[b, p * sb : (p + 1) * sb, cols] = attended[d, b, 0:sb]
            start = prompts * sb + p * pb
            block_rows[b, start : start + pb, cols] = attended[d, b, sb : sb + pb]

    def piece(g, o):
        b, half = g // 2, g % 2
        row = 0 if by_cols else o * crows
        col = (2 * o + half if by_cols else half) * ccols
        return b, slice(row, row + crows), slice(col, col + ccols)

    def shift_right(g, o, to):
        return remote(
            right_out.at[g, o], right_in.at[g, o], right_ssem.at[g, o], right_rsem.at[g, o], {"head": to}
        )

    def shift_left(g, o, to):
        return remote(
            left_out.at[g, o], left_in.at[g, o], left_ssem.at[g, o], left_rsem.at[g, o], {"head": to}
        )

    def share_right(g, o, to):
        rows = shared.at[g, o]
        return remote(rows, rows, agr_ssem.at[g, o], ag_rsem.at[g, o], {"head": to})

    def share_left(g, o, to):
        rows = shared.at[g, o]
        return remote(rows, rows, agl_ssem.at[g, o], ag_rsem.at[g, o], {"head": to})

    def when_group(g):
        return pl.when((g >= 0) & (g < groups))

    def project(g):
        for o in range(heads):
            b, rows, cols = piece(g, o)
            part[g, o] = jnp.dot(
                block_rows[b, rows], weight[:, cols], preferred_element_type=F32
            )

    def hop(tick):
        g = tick - z

        @when_group(g)
        def _():
            for o in range(heads - 1, 0, -1):

                @pl.when(z == 0)
                def _():
                    right_out[g, o] = part[g, o].astype(BF16)
                    shift_right(g, o, z + 1).start()

                @pl.when((z > 0) & (z < o))
                def _():
                    shift_right(g, o, z - 1).wait_recv()
                    right_out[g, o] = (part[g, o] + right_in[g, o].astype(F32)).astype(BF16)
                    shift_right(g, o, z + 1).start()

        h = tick - (heads - 1 - z)

        @when_group(h)
        def _():
            for o in range(heads - 1):

                @pl.when(z == heads - 1)
                def _():
                    left_out[h, o] = part[h, o].astype(BF16)
                    shift_left(h, o, z - 1).start()

                @pl.when((z < heads - 1) & (z > o))
                def _():
                    shift_left(h, o, z + 1).wait_recv()
                    left_out[h, o] = (part[h, o] + left_in[h, o].astype(F32)).astype(BF16)
                    shift_left(h, o, z - 1).start()

    def ready(o):
        return jnp.maximum(o, heads - 1 - o)

    def finish(tick):
        g = tick - ready(z)

        @when_group(g)
        def _():
            @pl.when(z == 0)
            def _():
                shift_left(g, z, z + 1).wait_recv()
                shared[g, z] = (part[g, z] + left_in[g, z].astype(F32)).astype(BF16)
                share_right(g, z, z + 1).start()

            @pl.when(z == heads - 1)
            def _():
                shift_right(g, z, z - 1).wait_recv()
                shared[g, z] = (part[g, z] + right_in[g, z].astype(F32)).astype(BF16)
                share_left(g, z, z - 1).start()

            @pl.when((z > 0) & (z < heads - 1))
            def _():
                shift_right(g, z, z - 1).wait_recv()
                shift_left(g, z, z + 1).wait_recv()
                shared[g, z] = (
                    part[g, z] + right_in[g, z].astype(F32) + left_in[g, z].astype(F32)
                ).astype(BF16)
                share_right(g, z, z + 1).start()
                share_left(g, z, z - 1).start()

    def relay(tick):
        for k in range(1, heads):
            o = z - k
            g = tick - ready(o) - k

            @pl.when((o >= 0) & (g >= 0) & (g < groups))
            def _():
                share_right(g, o, z - 1).wait_recv()

                @pl.when(z < heads - 1)
                def _():
                    share_right(g, o, z + 1).start()

            q = z + k
            h = tick - ready(q) - k

            @pl.when((q < heads) & (h >= 0) & (h < groups))
            def _():
                share_left(h, q, z + 1).wait_recv()

                @pl.when(z > 0)
                def _():
                    share_left(h, q, z - 1).start()

    def store(g, o):
        b, rows, cols = piece(g, o)
        return pltpu.make_async_copy(
            shared.at[g, o], summed.at[b, rows, cols], done_sem.at[g, o]
        )

    def tick(t):
        if t < groups:
            project(t)
        hop(t)
        finish(t)
        relay(t)
        g = t - 2 * (heads - 1)
        if g >= 0:
            for o in range(heads):
                store(g, o).start()

    for b in range(nb):
        attend_half(b, 0)
        if b == 0:
            load_weight.wait()
        if b >= 1:
            forward_all(b - 1)
        if b >= 2:
            tick(2 * (b - 2) + 1)
        attend_half(b, 1)
        to_sibling(b).start()
        for e in range(1, chips):
            to_far(e, b).start()
        if b >= 1:
            collect(b - 1)
            tick(2 * (b - 1))
    forward_all(nb - 1)
    tick(2 * (nb - 2) + 1)
    collect(nb - 1)
    for t in range(2 * (nb - 1), groups + 2 * (heads - 1)):
        tick(t)

    for d in range(1, ctx):
        send_queries(d).wait_send()
        send_span(d).wait_send()
        send_keys(d).wait_send()
    for b in range(nb):
        to_sibling(b).wait_send()
        for e in range(1, chips):
            to_far(e, b).wait_send()
            forward(e, b).wait_send()
    for g in range(groups):
        for o in range(heads):

            @pl.when(z < o)
            def _():
                shift_right(g, o, z + 1).wait_send()

            @pl.when(z > o)
            def _():
                shift_left(g, o, z - 1).wait_send()

            @pl.when((o <= z) & (z < heads - 1))
            def _():
                share_right(g, o, z + 1).wait_send()

            @pl.when((o >= z) & (z > 0))
            def _():
                share_left(g, o, z - 1).wait_send()

            store(g, o).wait()


def place_rows(dims, place, summed, span_out, decode_out, decode_rows):
    prompts, share, per_block, ctx, span_dev, sb, pb, picked, nb = dims
    span = ctx * span_dev
    for b in range(nb):
        for p in range(prompts):
            for n in range(per_block):
                c = (p * share + b * per_block + n) % ctx
                to = p * span + c * span_dev
                start = p * sb + n * span_dev
                span_out[to : to + span_dev] = summed[b, start : start + span_dev]
            start = prompts * sb + p * pb
            to = p * picked + b * pb
            decode_rows[to : to + pb] = summed[b, start : start + pb]
    decode_out[...] = lax.dot_general(
        place[...], decode_rows[...], (((0,), (0,)), ((), ())), preferred_element_type=F32
    ).astype(BF16)


def shards(
    ctx,
    heads,
    span_query,
    span_key,
    span_value,
    prefix_key,
    prefix_value,
    page_table,
    decode_query,
    decode_key,
    decode_value,
    sample_prompt,
    out_weight,
):
    prompts, span_dev, heads_dev, hd = span_query.shape
    kvh = span_key.shape[2]
    steps, samples_dev = decode_query.shape[:2]
    slots, page = prefix_key.shape[:2]
    pages = page_table.shape[1]
    samples = sample_prompt.shape[0]
    each = samples // prompts
    qh = heads_dev * prompts // ctx
    dec_dev = steps * samples_dev
    span = ctx * span_dev
    picked = each * steps
    features, columns = out_weight.shape
    nb = 4
    groups = 2 * nb
    brows = (prompts * span + steps * samples) // nb
    by_cols = columns // heads >= 256
    crows = brows if by_cols else brows // heads
    ccols = (columns // heads if by_cols else columns) // 2

    dims = (
        ctx,
        heads,
        prompts,
        kvh,
        heads_dev,
        pages,
        page,
        span_dev,
        steps,
        samples_dev,
        each,
        qh,
        nb,
        by_cols,
    )
    kv_rows = 2 * pages * page + 2 * span_dev + 2 * dec_dev
    q_rows = qh * (span_dev + dec_dev)
    vmem = pl.BlockSpec(memory_space=pltpu.VMEM)
    dma = pltpu.SemaphoreType.DMA
    sums = (groups, heads, crows, ccols)
    summed, place = pl.pallas_call(
        functools.partial(kernel, dims),
        out_shape=(
            jax.ShapeDtypeStruct((nb, brows, columns), BF16),
            jax.ShapeDtypeStruct((prompts * picked, steps * samples), BF16),
        ),
        in_specs=[pl.BlockSpec(memory_space=pltpu.SMEM)]
        + [vmem] * 9
        + [pl.BlockSpec(memory_space=pl.ANY)],
        out_specs=(pl.BlockSpec(memory_space=pl.ANY), vmem),
        scratch_shapes=[
            pltpu.VMEM((prompts * kvh, kv_rows, hd), BF16),
            pltpu.VMEM((ctx, q_rows, hd), BF16),
            pltpu.VMEM((ctx, kv_rows, hd), BF16),
            pltpu.VMEM((ctx, q_rows, hd), BF16),
            pltpu.VMEM((ctx, nb, (span + picked) // nb, qh * hd), BF16),
            pltpu.VMEM((nb, brows, features), BF16),
            pltpu.VMEM((features, columns), BF16),
            pltpu.VMEM(sums, F32),
            pltpu.VMEM(sums, BF16),
            pltpu.VMEM(sums, BF16),
            pltpu.VMEM(sums, BF16),
            pltpu.VMEM(sums, BF16),
            pltpu.VMEM(sums, BF16),
            dma((ctx,)),
            dma((ctx,)),
            dma((ctx,)),
            dma((ctx,)),
            dma((ctx,)),
            dma((ctx,)),
            dma((2,)),
            dma((nb,)),
            dma((ctx // 2, nb)),
            dma((ctx // 2, nb)),
            dma((ctx, nb)),
            dma((1,)),
        ]
        + [dma((groups, heads))] * 8,
        compiler_params=pltpu.CompilerParams(
            collective_id=0, has_side_effects=True, vmem_limit_bytes=58 * 1024 * 1024
        ),
        cost_estimate=pl.CostEstimate(
            flops=2 * prompts * span * features * columns,
            bytes_accessed=16 * 1024 * 1024,
            transcendentals=0,
        ),
    )(
        page_table,
        sample_prompt.reshape(1, samples),
        prefix_key.reshape(slots, page * kvh, hd),
        prefix_value.reshape(slots, page * kvh, hd),
        span_query.reshape(-1, hd),
        decode_query.reshape(-1, hd),
        span_key.reshape(-1, hd),
        span_value.reshape(-1, hd),
        decode_key.reshape(-1, hd),
        decode_value.reshape(-1, hd),
        out_weight,
    )
    width = math.gcd(columns, 512)
    place_dims = (
        prompts,
        ctx // prompts,
        ctx // nb,
        ctx,
        span_dev,
        span // nb,
        picked // nb,
        picked,
        nb,
    )
    span_out, decode_out = pl.pallas_call(
        functools.partial(place_rows, place_dims),
        grid=(columns // width,),
        out_shape=(
            jax.ShapeDtypeStruct((prompts * span, columns), BF16),
            jax.ShapeDtypeStruct((steps * samples, columns), BF16),
        ),
        in_specs=[
            pl.BlockSpec((prompts * picked, steps * samples), lambda i: (0, 0)),
            pl.BlockSpec((nb, brows, width), lambda i: (0, 0, i)),
        ],
        out_specs=(
            pl.BlockSpec((prompts * span, width), lambda i: (0, i)),
            pl.BlockSpec((steps * samples, width), lambda i: (0, i)),
        ),
        scratch_shapes=[pltpu.VMEM((prompts * picked, width), BF16)],
        compiler_params=pltpu.CompilerParams(vmem_limit_bytes=58 * 1024 * 1024),
        cost_estimate=pl.CostEstimate(
            flops=2 * (steps * samples) ** 2 * columns,
            bytes_accessed=4 * brows * nb * columns,
            transcendentals=0,
        ),
    )(place, summed)
    return (
        span_out.reshape(prompts, span, columns),
        decode_out.reshape(steps, samples, columns),
    )


def solution(mesh):
    return jax.shard_map(
        functools.partial(shards, mesh.shape["ctx"], mesh.shape["head"]),
        mesh=mesh,
        in_specs=(
            P("groups", "ctx", "head", None),
            P("groups", "ctx", "head", None),
            P("groups", "ctx", "head", None),
            P(("groups", "ctx"), None, "head", None),
            P(("groups", "ctx"), None, "head", None),
            P("groups", "ctx"),
            P("groups", "ctx", "head", None),
            P("groups", "ctx", "head", None),
            P("groups", "ctx", "head", None),
            P("groups"),
            P("head", "ctx"),
        ),
        out_specs=(P("groups", None, "ctx"), P("groups", None, "ctx")),
        check_vma=False,
    )
```

```python
import functools
import math

import jax
import jax.numpy as jnp
from jax import lax
from jax.experimental import pallas as pl
from jax.experimental.pallas import tpu as pltpu
from jax.sharding import PartitionSpec as P

MESH = pl.DeviceIdType.MESH
F32 = jnp.float32
BF16 = jnp.bfloat16
masked_bias = -1e30


def div(x, n):
    if n & (n - 1):
        return x // n
    return lax.shift_right_logical(x, jnp.int32(n.bit_length() - 1))


def mod(x, n):
    if n & (n - 1):
        return x % n
    return x & (n - 1)


def iotas(rows, cols):
    shape = (rows, cols)
    return (
        lax.broadcasted_iota(jnp.int32, shape, 0),
        lax.broadcasted_iota(jnp.int32, shape, 1),
    )


def one_hot(mask):
    return jnp.where(mask, 1.0, 0.0).astype(BF16)


def exact(left, right):
    return jnp.dot(left, right, preferred_element_type=F32).astype(BF16)


def heads_first(outer, inner):
    i, j = iotas(outer * inner, outer * inner)
    return one_hot(j == mod(i, outer) * inner + div(i, outer))


def remote(src, dst, send, recv, device):
    return pltpu.make_async_remote_copy(
        src_ref=src,
        dst_ref=dst,
        send_sem=send,
        recv_sem=recv,
        device_id=device,
        device_id_type=MESH,
    )


def kernel(
    dims,
    table,
    prompt_in,
    keys_in,
    values_in,
    span_q_in,
    decode_q_in,
    span_k_in,
    span_v_in,
    decode_k_in,
    decode_v_in,
    weight_in,
    summed,
    place_out,
    kv_send,
    q_send,
    kv_held,
    q_held,
    attended,
    block_rows,
    weight,
    part,
    right_out,
    left_out,
    right_in,
    left_in,
    shared,
    kv_ssem,
    kv_rsem,
    q_ssem,
    q_rsem,
    s_ssem,
    s_rsem,
    own_sem,
    sib_ssem,
    far_ssem,
    fwd_ssem,
    att_rsem,
    weight_sem,
    right_ssem,
    right_rsem,
    left_ssem,
    left_rsem,
    agr_ssem,
    agl_ssem,
    ag_rsem,
    done_sem,
):
    (
        ctx,
        heads,
        prompts,
        kvh,
        heads_dev,
        pages,
        page,
        span_dev,
        steps,
        samples_dev,
        each,
        qh,
        nb,
        by_cols,
    ) = dims
    me = lax.axis_index("ctx")
    z = lax.axis_index("head")
    share = ctx // prompts
    hd = 128
    chips = ctx // 2
    prefix = pages * page
    dec_dev = steps * samples_dev
    samples = ctx * samples_dev
    span = ctx * span_dev
    picked = each * steps
    sb, pb = span // nb, picked // nb
    groups, unused, crows, ccols = shared.shape

    load_weight = pltpu.make_async_copy(weight_in, weight, weight_sem.at[0])
    load_weight.start()

    barrier = pltpu.get_barrier_semaphore()
    for d in range(1, ctx):
        pl.semaphore_signal(
            barrier, inc=1, device_id={"ctx": lax.rem(me + d, ctx)}, device_id_type=MESH
        )

    @pl.when(z > 0)
    def _():
        pl.semaphore_signal(barrier, inc=1, device_id={"head": z - 1}, device_id_type=MESH)

    @pl.when(z < heads - 1)
    def _():
        pl.semaphore_signal(barrier, inc=1, device_id={"head": z + 1}, device_id_type=MESH)

    order = heads_first(span_dev, heads_dev)
    block = span_dev * heads_dev
    span_rows = [
        exact(order, span_q_in[p * block : (p + 1) * block]) for p in range(prompts)
    ]
    dec_rows = exact(heads_first(dec_dev, heads_dev), decode_q_in[...])
    for d in range(ctx):
        p, r = d // share, d % share
        q_send[d, 0 : qh * span_dev] = span_rows[p][r * qh * span_dev : (r + 1) * qh * span_dev]
        q_send[d, qh * span_dev :] = dec_rows[r * qh * dec_dev : (r + 1) * qh * dec_dev]

    pl.semaphore_wait(
        barrier, ctx - 1 + jnp.where(z > 0, 1, 0) + jnp.where(z < heads - 1, 1, 0)
    )

    def unit_of(d):
        return d // share * kvh + d % share * kvh // share

    core_pair = me + 1 - 2 * lax.rem(me, 2)
    q_span = pl.ds(0, qh * span_dev)
    q_dec = pl.ds(qh * span_dev, qh * dec_dev)

    def send_queries(d):
        to = lax.rem(me + d, ctx)
        return remote(
            q_send.at[to, q_dec], q_held.at[me, q_dec], q_ssem.at[d], q_rsem.at[me], {"ctx": to}
        )

    def send_span(d):
        to = lax.rem(me + d, ctx)
        return remote(
            q_send.at[to, q_span], q_held.at[me, q_span], s_ssem.at[d], s_rsem.at[me], {"ctx": to}
        )

    def send_keys(d):
        to = lax.rem(me + d, ctx)
        return remote(
            kv_send.at[unit_of(to)], kv_held.at[me], kv_ssem.at[d], kv_rsem.at[me], {"ctx": to}
        )

    for d in range(1, ctx):
        send_queries(d).start()

        @pl.when(lax.rem(me + d, ctx) == core_pair)
        def _():
            send_span(d).start()

    def split(outer, keys, values):
        both = jnp.concatenate([keys, values], axis=1)
        if kvh == 1:
            return both
        return exact(heads_first(outer, kvh), both)

    base = 2 * prefix
    for p in range(prompts):
        for j in range(pages):
            slot = table[p, j]
            both = split(page, keys_in[slot], values_in[slot])
            for k in range(kvh):
                u = p * kvh + k
                rows = both[k * page : (k + 1) * page]
                kv_send[u, j * page : (j + 1) * page] = rows[:, :hd]
                kv_send[u, prefix + j * page : prefix + (j + 1) * page] = rows[:, hd:]
        size = span_dev * kvh
        mine = slice(p * size, (p + 1) * size)
        span_both = split(span_dev, span_k_in[mine], span_v_in[mine])
        dec_both = split(dec_dev, decode_k_in[...], decode_v_in[...])
        for k in range(kvh):
            u = p * kvh + k
            at = base
            for both, size in ((span_both, span_dev), (dec_both, dec_dev)):
                rows = both[k * size : (k + 1) * size]
                kv_send[u, at : at + size] = rows[:, :hd]
                kv_send[u, at + size : at + 2 * size] = rows[:, hd:]
                at += 2 * size

    for d in range(1, ctx):
        send_keys(d).start()
    own = (
        pltpu.make_async_copy(q_send.at[me], q_held.at[me], own_sem.at[0]),
        pltpu.make_async_copy(kv_send.at[unit_of(me)], kv_held.at[me], own_sem.at[1]),
    )
    for copy in own:
        copy.start()

    prompt_row = jnp.broadcast_to(prompt_in[...], (8, samples))
    i, j = iotas(samples, samples)
    earlier = one_hot(i < j)
    code = jnp.zeros((8, samples), F32)
    for p in range(prompts):
        here = one_hot(prompt_row == p)
        rank = jnp.dot(here, earlier, preferred_element_type=F32)
        code = code + here.astype(F32) * (rank + p * each)
    code = code.astype(BF16)

    i, j = iotas(samples, ctx * dec_dev)
    spread = one_hot(i == div(j, dec_dev) * samples_dev + mod(j, samples_dev))
    col_code = jnp.dot(code, spread, preferred_element_type=F32)[0:1]
    i, j = iotas(picked, ctx * dec_dev)
    wanted = (div(i, steps) + me // share * each).astype(F32)
    same = jnp.where(col_code == wanted, 1, 0)
    later = mod(i, steps) - mod(div(j, samples_dev), steps)
    pick = one_hot((same == 1) & (later == 0))
    own_bias = jnp.where((same == 1) & (later >= 0), 0.0, masked_bias)

    i, j = iotas(samples, steps * samples)
    col_code = jnp.dot(code, one_hot(i == mod(j, samples)), preferred_element_type=F32)[0:1]
    i, j = iotas(prompts * picked, steps * samples)
    same = jnp.where(col_code == div(i, steps).astype(F32), 1, 0)
    place_out[...] = one_hot((same == 1) & (div(j, samples) == mod(i, steps)))

    for copy in own:
        copy.wait()
    for d in range(1, ctx):
        at = lax.rem(me + d, ctx)
        rows = q_held.at[at, q_dec]
        remote(rows, rows, q_ssem.at[d], q_rsem.at[at], {"ctx": at}).wait_recv()
    dq = jnp.concatenate(
        [
            jnp.concatenate(
                [
                    q_held[c, qh * span_dev + g * dec_dev : qh * span_dev + (g + 1) * dec_dev]
                    for c in range(ctx)
                ],
                axis=0,
            )
            for g in range(qh)
        ],
        axis=1,
    )
    dq = exact(pick, dq)
    for d in range(1, ctx):
        at = lax.rem(me + d, ctx)
        remote(
            kv_held.at[at], kv_held.at[at], kv_ssem.at[d], kv_rsem.at[at], {"ctx": at}
        ).wait_recv()
    for d in range(1, ctx):

        @pl.when(lax.rem(me + d, ctx) != core_pair)
        def _():
            send_span(d).start()

    factor = math.log2(math.e) / math.sqrt(hd)
    at = base
    extra = []
    for width in (span_dev, span_dev, dec_dev, dec_dev):
        extra.append([kv_held[c, at : at + width] for c in range(ctx)])
        at += width
    extra_keys = jnp.concatenate(extra[0] + extra[2], axis=0)
    extra_values = jnp.concatenate(extra[1] + extra[3], axis=0)

    def far(e):
        return lax.rem(me + 2 * e, ctx)

    def gather_copy(source, b, sem, to):
        rows = attended.at[source, b]
        return remote(rows, rows, sem, att_rsem.at[source, b], {"ctx": to})

    def to_sibling(b):
        return gather_copy(me, b, sib_ssem.at[b], core_pair)

    def to_far(e, b):
        return gather_copy(me, b, far_ssem.at[e, b], far(e))

    def forward(e, b):
        return gather_copy(far(e), b, fwd_ssem.at[e, b], core_pair)

    def forward_all(b):
        for e in range(1, chips):
            forward(e, b).wait_recv()
            forward(e, b).start()

    def dot_keys(queries, keys):
        return lax.dot_general(queries, keys, (((1,), (1,)), ((), ())), preferred_element_type=F32)

    def attend(queries, bias):
        scores = [dot_keys(queries, kv_held[c, 0:prefix]) for c in range(ctx)]
        last = dot_keys(queries, extra_keys) + bias
        top = jnp.max(last, axis=1, keepdims=True)
        for s in scores:
            top = jnp.maximum(top, jnp.max(s, axis=1, keepdims=True))
        shift = top * factor
        w = jnp.exp2(last * factor - shift)
        total = jnp.sum(w, axis=1, keepdims=True)
        mixed = jnp.dot(w.astype(BF16), extra_values, preferred_element_type=F32)
        for c, s in enumerate(scores):
            w = jnp.exp2(s * factor - shift)
            total = total + jnp.sum(w, axis=1, keepdims=True)
            mixed = mixed + jnp.dot(
                w.astype(BF16), kv_held[c, prefix : 2 * prefix], preferred_element_type=F32
            )
        return (mixed / total).astype(BF16)

    per_block = ctx // nb

    def attend_half(b, half):
        split_at = (qh + 1) // 2
        chosen = range(0, split_at) if half == 0 else range(split_at, qh)
        count = len(chosen)
        if count == 0:
            return
        sources = [
            lax.rem(me // share * share + b * per_block + n, ctx) for n in range(per_block)
        ]
        if half == 0:
            for c in sources:

                @pl.when(c != me)
                def _():
                    rows = q_held.at[c, q_span]
                    remote(rows, rows, s_ssem.at[0], s_rsem.at[c], {"ctx": c}).wait_recv()

        queries = [
            q_held[c, g * span_dev : (g + 1) * span_dev] for g in chosen for c in sources
        ] + [dq[b * pb : (b + 1) * pb, g * hd : (g + 1) * hd] for g in chosen]
        i, j = iotas(span_dev, span)
        span_part = jnp.concatenate(
            [
                jnp.concatenate(
                    [
                        jnp.where(j <= i + c * span_dev, 0.0, masked_bias),
                        jnp.full((span_dev, ctx * dec_dev), masked_bias, F32),
                    ],
                    axis=1,
                )
                for c in sources
            ],
            axis=0,
        )
        dec_part = jnp.concatenate(
            [jnp.zeros((pb, span), F32), own_bias[b * pb : (b + 1) * pb]], axis=1
        )
        bias = jnp.concatenate([span_part] * count + [dec_part] * count, axis=0)
        mixed = attend(jnp.concatenate(queries, axis=0), bias)
        for n, g in enumerate(chosen):
            cols = slice(g * hd, (g + 1) * hd)
            attended[me, b, 0:sb, cols] = mixed[n * sb : (n + 1) * sb]
            start = count * sb + n * pb
            attended[me, b, sb : sb + pb, cols] = mixed[start : start + pb]

    def collect(b):
        gather_copy(core_pair, b, sib_ssem.at[b], core_pair).wait_recv()
        for e in range(1, chips):
            gather_copy(
                lax.rem(core_pair + 2 * e, ctx), b, fwd_ssem.at[e, b], core_pair
            ).wait_recv()
        for d in range(ctx):
            p, r = d // share, d % share
            cols = slice(r * qh * hd, (r + 1) * qh * hd)
            block_rows[b, p * sb : (p + 1) * sb, cols] = attended[d, b, 0:sb]
            start = prompts * sb + p * pb
            block_rows[b, start : start + pb, cols] = attended[d, b, sb : sb + pb]

    def piece(g, o):
        b, part_of = g // 4, g % 4
        row = 0 if by_cols else o * crows
        col = (4 * o + part_of if by_cols else part_of) * ccols
        return b, slice(row, row + crows), slice(col, col + ccols)

    def shift_right(g, o, to):
        return remote(
            right_out.at[g, o], right_in.at[g, o], right_ssem.at[g, o], right_rsem.at[g, o], {"head": to}
        )

    def shift_left(g, o, to):
        return remote(
            left_out.at[g, o], left_in.at[g, o], left_ssem.at[g, o], left_rsem.at[g, o], {"head": to}
        )

    def share_right(g, o, to):
        rows = shared.at[g, o]
        return remote(rows, rows, agr_ssem.at[g, o], ag_rsem.at[g, o], {"head": to})

    def share_left(g, o, to):
        rows = shared.at[g, o]
        return remote(rows, rows, agl_ssem.at[g, o], ag_rsem.at[g, o], {"head": to})

    def when_group(g):
        return pl.when((g >= 0) & (g < groups))

    def project(g):
        for o in range(heads):
            b, rows, cols = piece(g, o)
            part[g, o] = jnp.dot(
                block_rows[b, rows], weight[:, cols], preferred_element_type=F32
            )

    def hop(tick):
        g = tick - z

        @when_group(g)
        def _():
            for o in range(heads - 1, 0, -1):

                @pl.when(z == 0)
                def _():
                    right_out[g, o] = part[g, o].astype(BF16)
                    shift_right(g, o, z + 1).start()

                @pl.when((z > 0) & (z < o))
                def _():
                    shift_right(g, o, z - 1).wait_recv()
                    right_out[g, o] = (part[g, o] + right_in[g, o].astype(F32)).astype(BF16)
                    shift_right(g, o, z + 1).start()

        h = tick - (heads - 1 - z)

        @when_group(h)
        def _():
            for o in range(heads - 1):

                @pl.when(z == heads - 1)
                def _():
                    left_out[h, o] = part[h, o].astype(BF16)
                    shift_left(h, o, z - 1).start()

                @pl.when((z < heads - 1) & (z > o))
                def _():
                    shift_left(h, o, z + 1).wait_recv()
                    left_out[h, o] = (part[h, o] + left_in[h, o].astype(F32)).astype(BF16)
                    shift_left(h, o, z - 1).start()

    def ready(o):
        return jnp.maximum(o, heads - 1 - o)

    def finish(tick):
        g = tick - ready(z)

        @when_group(g)
        def _():
            @pl.when(z == 0)
            def _():
                shift_left(g, z, z + 1).wait_recv()
                shared[g, z] = (part[g, z] + left_in[g, z].astype(F32)).astype(BF16)
                share_right(g, z, z + 1).start()

            @pl.when(z == heads - 1)
            def _():
                shift_right(g, z, z - 1).wait_recv()
                shared[g, z] = (part[g, z] + right_in[g, z].astype(F32)).astype(BF16)
                share_left(g, z, z - 1).start()

            @pl.when((z > 0) & (z < heads - 1))
            def _():
                shift_right(g, z, z - 1).wait_recv()
                shift_left(g, z, z + 1).wait_recv()
                shared[g, z] = (
                    part[g, z] + right_in[g, z].astype(F32) + left_in[g, z].astype(F32)
                ).astype(BF16)
                share_right(g, z, z + 1).start()
                share_left(g, z, z - 1).start()

    def relay(tick):
        for k in range(1, heads):
            o = z - k
            g = tick - ready(o) - k

            @pl.when((o >= 0) & (g >= 0) & (g < groups))
            def _():
                share_right(g, o, z - 1).wait_recv()

                @pl.when(z < heads - 1)
                def _():
                    share_right(g, o, z + 1).start()

            q = z + k
            h = tick - ready(q) - k

            @pl.when((q < heads) & (h >= 0) & (h < groups))
            def _():
                share_left(h, q, z + 1).wait_recv()

                @pl.when(z > 0)
                def _():
                    share_left(h, q, z - 1).start()

    def store(g, o):
        b, rows, cols = piece(g, o)
        return pltpu.make_async_copy(
            shared.at[g, o], summed.at[b, rows, cols], done_sem.at[g, o]
        )

    def tick(t):
        if t < groups:
            project(t)
        hop(t)
        finish(t)
        relay(t)
        g = t - 2 * (heads - 1)
        if g >= 0:
            for o in range(heads):
                store(g, o).start()

    for b in range(nb):
        attend_half(b, 0)
        if b == 0:
            load_weight.wait()
        if b >= 1:
            forward_all(b - 1)
        if b >= 2:
            tick(4 * (b - 2) + 2)
            tick(4 * (b - 2) + 3)
        attend_half(b, 1)
        to_sibling(b).start()
        for e in range(1, chips):
            to_far(e, b).start()
        if b >= 1:
            collect(b - 1)
            tick(4 * (b - 1))
            tick(4 * (b - 1) + 1)
    forward_all(nb - 1)
    tick(4 * (nb - 2) + 2)
    tick(4 * (nb - 2) + 3)
    collect(nb - 1)
    for t in range(4 * (nb - 1), groups + 2 * (heads - 1)):
        tick(t)

    for d in range(1, ctx):
        send_queries(d).wait_send()
        send_span(d).wait_send()
        send_keys(d).wait_send()
    for b in range(nb):
        to_sibling(b).wait_send()
        for e in range(1, chips):
            to_far(e, b).wait_send()
            forward(e, b).wait_send()
    for g in range(groups):
        for o in range(heads):

            @pl.when(z < o)
            def _():
                shift_right(g, o, z + 1).wait_send()

            @pl.when(z > o)
            def _():
                shift_left(g, o, z - 1).wait_send()

            @pl.when((o <= z) & (z < heads - 1))
            def _():
                share_right(g, o, z + 1).wait_send()

            @pl.when((o >= z) & (z > 0))
            def _():
                share_left(g, o, z - 1).wait_send()

            store(g, o).wait()


def place_rows(dims, place, summed, span_out, decode_out, decode_rows):
    prompts, share, per_block, ctx, span_dev, sb, pb, picked, nb = dims
    span = ctx * span_dev
    for b in range(nb):
        for p in range(prompts):
            for n in range(per_block):
                c = (p * share + b * per_block + n) % ctx
                to = p * span + c * span_dev
                start = p * sb + n * span_dev
                span_out[to : to + span_dev] = summed[b, start : start + span_dev]
            start = prompts * sb + p * pb
            to = p * picked + b * pb
            decode_rows[to : to + pb] = summed[b, start : start + pb]
    decode_out[...] = lax.dot_general(
        place[...], decode_rows[...], (((0,), (0,)), ((), ())), preferred_element_type=F32
    ).astype(BF16)


def shards(
    ctx,
    heads,
    span_query,
    span_key,
    span_value,
    prefix_key,
    prefix_value,
    page_table,
    decode_query,
    decode_key,
    decode_value,
    sample_prompt,
    out_weight,
):
    prompts, span_dev, heads_dev, hd = span_query.shape
    kvh = span_key.shape[2]
    steps, samples_dev = decode_query.shape[:2]
    slots, page = prefix_key.shape[:2]
    pages = page_table.shape[1]
    samples = sample_prompt.shape[0]
    each = samples // prompts
    qh = heads_dev * prompts // ctx
    dec_dev = steps * samples_dev
    span = ctx * span_dev
    picked = each * steps
    features, columns = out_weight.shape
    nb = 4
    groups = 4 * nb
    brows = (prompts * span + steps * samples) // nb
    by_cols = columns // heads >= 512
    crows = brows if by_cols else brows // heads
    ccols = (columns // heads if by_cols else columns) // 4

    dims = (
        ctx,
        heads,
        prompts,
        kvh,
        heads_dev,
        pages,
        page,
        span_dev,
        steps,
        samples_dev,
        each,
        qh,
        nb,
        by_cols,
    )
    kv_rows = 2 * pages * page + 2 * span_dev + 2 * dec_dev
    q_rows = qh * (span_dev + dec_dev)
    vmem = pl.BlockSpec(memory_space=pltpu.VMEM)
    dma = pltpu.SemaphoreType.DMA
    sums = (groups, heads, crows, ccols)
    summed, place = pl.pallas_call(
        functools.partial(kernel, dims),
        out_shape=(
            jax.ShapeDtypeStruct((nb, brows, columns), BF16),
            jax.ShapeDtypeStruct((prompts * picked, steps * samples), BF16),
        ),
        in_specs=[pl.BlockSpec(memory_space=pltpu.SMEM)]
        + [vmem] * 9
        + [pl.BlockSpec(memory_space=pl.ANY)],
        out_specs=(pl.BlockSpec(memory_space=pl.ANY), vmem),
        scratch_shapes=[
            pltpu.VMEM((prompts * kvh, kv_rows, hd), BF16),
            pltpu.VMEM((ctx, q_rows, hd), BF16),
            pltpu.VMEM((ctx, kv_rows, hd), BF16),
            pltpu.VMEM((ctx, q_rows, hd), BF16),
            pltpu.VMEM((ctx, nb, (span + picked) // nb, qh * hd), BF16),
            pltpu.VMEM((nb, brows, features), BF16),
            pltpu.VMEM((features, columns), BF16),
            pltpu.VMEM(sums, F32),
            pltpu.VMEM(sums, BF16),
            pltpu.VMEM(sums, BF16),
            pltpu.VMEM(sums, BF16),
            pltpu.VMEM(sums, BF16),
            pltpu.VMEM(sums, BF16),
            dma((ctx,)),
            dma((ctx,)),
            dma((ctx,)),
            dma((ctx,)),
            dma((ctx,)),
            dma((ctx,)),
            dma((2,)),
            dma((nb,)),
            dma((ctx // 2, nb)),
            dma((ctx // 2, nb)),
            dma((ctx, nb)),
            dma((1,)),
        ]
        + [dma((groups, heads))] * 8,
        compiler_params=pltpu.CompilerParams(
            collective_id=0, has_side_effects=True, vmem_limit_bytes=58 * 1024 * 1024
        ),
        cost_estimate=pl.CostEstimate(
            flops=2 * prompts * span * features * columns,
            bytes_accessed=16 * 1024 * 1024,
            transcendentals=0,
        ),
    )(
        page_table,
        sample_prompt.reshape(1, samples),
        prefix_key.reshape(slots, page * kvh, hd),
        prefix_value.reshape(slots, page * kvh, hd),
        span_query.reshape(-1, hd),
        decode_query.reshape(-1, hd),
        span_key.reshape(-1, hd),
        span_value.reshape(-1, hd),
        decode_key.reshape(-1, hd),
        decode_value.reshape(-1, hd),
        out_weight,
    )
    width = math.gcd(columns, 512)
    place_dims = (
        prompts,
        ctx // prompts,
        ctx // nb,
        ctx,
        span_dev,
        span // nb,
        picked // nb,
        picked,
        nb,
    )
    span_out, decode_out = pl.pallas_call(
        functools.partial(place_rows, place_dims),
        grid=(columns // width,),
        out_shape=(
            jax.ShapeDtypeStruct((prompts * span, columns), BF16),
            jax.ShapeDtypeStruct((steps * samples, columns), BF16),
        ),
        in_specs=[
            pl.BlockSpec((prompts * picked, steps * samples), lambda i: (0, 0)),
            pl.BlockSpec((nb, brows, width), lambda i: (0, 0, i)),
        ],
        out_specs=(
            pl.BlockSpec((prompts * span, width), lambda i: (0, i)),
            pl.BlockSpec((steps * samples, width), lambda i: (0, i)),
        ),
        scratch_shapes=[pltpu.VMEM((prompts * picked, width), BF16)],
        compiler_params=pltpu.CompilerParams(vmem_limit_bytes=58 * 1024 * 1024),
        cost_estimate=pl.CostEstimate(
            flops=2 * (steps * samples) ** 2 * columns,
            bytes_accessed=4 * brows * nb * columns,
            transcendentals=0,
        ),
    )(place, summed)
    return (
        span_out.reshape(prompts, span, columns),
        decode_out.reshape(steps, samples, columns),
    )


def solution(mesh):
    return jax.shard_map(
        functools.partial(shards, mesh.shape["ctx"], mesh.shape["head"]),
        mesh=mesh,
        in_specs=(
            P("groups", "ctx", "head", None),
            P("groups", "ctx", "head", None),
            P("groups", "ctx", "head", None),
            P(("groups", "ctx"), None, "head", None),
            P(("groups", "ctx"), None, "head", None),
            P("groups", "ctx"),
            P("groups", "ctx", "head", None),
            P("groups", "ctx", "head", None),
            P("groups", "ctx", "head", None),
            P("groups"),
            P("head", "ctx"),
        ),
        out_specs=(P("groups", None, "ctx"), P("groups", None, "ctx")),
        check_vma=False,
    )
```
